256 devices in a mesh: view: 4 (over x_lo, core), seq: 64 (over y, z, x_hi).
Axes of the slice: x: 4 (x_hi: 2, x_lo: 2; x = x_hi * 2 + x_lo), y: 4, z: 8, core: 2. Of those that a mesh axis runs over, the one named last changes fastest.
Arguments:
- hidden_in: bfloat16 [4, 8192, 2048], P('view', 'seq'), may hold values from -6 to 6
- queries: bfloat16 [4, 8192, 2048], P('view', 'seq'), may hold values from -100 to 100
- keys: bfloat16 [4, 8192, 2048], P('view', 'seq'), may hold values from -4 to 4
- values: bfloat16 [4, 8192, 2048], P('view', 'seq'), may hold values from -6 to 6
- out_weight: bfloat16 [2048, 2048], replicated, may hold values from -0.125 to 0.125
- gate: bfloat16 [4, 2048], P('view'), may hold values from 0.5 to 1.5
Outputs:
- updated: bfloat16 [4, 8192, 2048], P('view', 'seq')
The draws below stay inside these ranges and needn't reach their ends.
All inputs are finite; a program needn't handle non-finite values.
Results may differ from the reference program's by a relative error of at most 0.015.
Values may be sent and summed in bfloat16 or wider, within the bound.
No kernel may reach another device: no remote copies, remote signals or barrier semaphores. Data moves between devices by JAX's collectives and lax.ppermute only.
A program may use at most 128 MiB of HBM per device.

```python
import jax
import jax.numpy as jnp
from jax import lax

HEADS = 16
HEAD_DIM = 128
D = 2048
VIEWS = 4
SEQ_LEN = 8192


def shared_keys(key):
    return jax.random.truncated_normal(jax.random.fold_in(key, 11), -4.0, 4.0, (VIEWS, SEQ_LEN, D), jnp.float32)


def draw_keys(key, part):
    base_keys = shared_keys(key)
    return base_keys.astype(jnp.bfloat16)


def draw_queries(key, part):
    key = jax.random.fold_in(key, 7)
    result = 2.5 * jax.random.truncated_normal(key, -4.0, 4.0, (VIEWS, SEQ_LEN, D), jnp.float32)
    return result.astype(jnp.bfloat16)


def block_scale(rng, dims, cuts, low, largest):
    level = 1.0
    for axis_at, shards_of in cuts:
        heights = jax.random.uniform(jax.random.fold_in(jax.random.fold_in(rng, 6), axis_at), (shards_of,), jnp.float32, low / len(cuts), largest / len(cuts))
        level = level * jnp.repeat(jnp.exp(heights), dims[axis_at] // shards_of).reshape((-1,) + (1,) * (len(dims) - 1 - axis_at))
    return level


def scatter_about(own_key, shape, deviation, limit, pieces=(), kind=jnp.bfloat16):
    drawn = jax.random.normal(own_key, shape, jnp.float32) * deviation
    if len(pieces) > 0:
        drawn = block_scale(own_key, shape, pieces, -0.22, 0.18) * drawn
    return jnp.clip(drawn, min=-limit, max=limit).astype(kind)


def setup_inputs(seed: int = 0) -> dict:
    key_list = jax.random.split(jax.random.key(seed), 7)
    return {
        "hidden_in": scatter_about(key_list[0], (VIEWS, SEQ_LEN, D), 1.0, 6.0, ((0, 4), (1, 64))),
        "queries": draw_queries(jax.random.fold_in(key_list[6], 71), 0),
        "keys": draw_keys(jax.random.fold_in(key_list[6], 71), 0),
        "values": scatter_about(key_list[3], (VIEWS, SEQ_LEN, D), 1.0, 6.0, ((0, 4), (1, 64))),
        "out_weight": scatter_about(key_list[4], (D, D), D ** -0.5, 0.125),
        "gate": jnp.clip(0.5 + 1.0 * jax.random.uniform(key_list[5], (VIEWS, D), jnp.float32) ** block_scale(key_list[5], (VIEWS, D), ((0, 4),), -0.2, 0.2), 0.5, 1.5).astype(jnp.bfloat16),
    }


def normalized(scores, axis):
    row_peak = jnp.max(scores, axis=axis, keepdims=True)
    expanded = jnp.exp(scores - row_peak)
    return (expanded / jnp.sum(expanded, axis=axis, keepdims=True)).astype(jnp.bfloat16)


def reference(hidden_in, queries, keys, values, out_weight, gate):
    score_scale = HEAD_DIM ** -0.5
    query_heads = queries.reshape(VIEWS, SEQ_LEN, HEADS, HEAD_DIM)
    key_heads = keys.reshape(VIEWS, SEQ_LEN, HEADS, HEAD_DIM)
    value_heads = values.reshape(VIEWS, SEQ_LEN, HEADS, HEAD_DIM)

    def flatten(array):
        return array.transpose(0, 2, 1, 3).reshape(VIEWS * HEADS, SEQ_LEN, HEAD_DIM)

    def one_head(items):
        query_rows, key_rows, value_rows = items
        scores = jnp.dot(query_rows, key_rows.T, preferred_element_type=jnp.float32) * score_scale
        row_peak = jnp.max(scores, axis=-1, keepdims=True)
        expanded = jnp.exp(scores - row_peak)
        row_total = jnp.sum(expanded, axis=-1, keepdims=True)
        summed = jnp.dot(expanded.astype(jnp.bfloat16), value_rows, preferred_element_type=jnp.float32)
        return (summed / row_total).astype(jnp.bfloat16)

    self_out = lax.map(one_head, (flatten(query_heads), flatten(key_heads), flatten(value_heads)))
    self_out = self_out.reshape(VIEWS, HEADS, SEQ_LEN, HEAD_DIM).transpose(0, 2, 1, 3).reshape(VIEWS, SEQ_LEN, D)
    cross_scores = jnp.einsum("aphd,bphd->apbh", query_heads.astype(jnp.float32), key_heads.astype(jnp.float32)) * score_scale
    cross_weights = normalized(cross_scores, 2)
    cross_out = jnp.einsum("apbh,bphd->aphd", cross_weights.astype(jnp.float32), value_heads.astype(jnp.float32))
    attended = (self_out.astype(jnp.float32) + cross_out.reshape(VIEWS, SEQ_LEN, D)).astype(jnp.bfloat16)
    projected = jnp.dot(attended.reshape(VIEWS * SEQ_LEN, D), out_weight, preferred_element_type=jnp.float32)
    projected = projected.reshape(VIEWS, SEQ_LEN, D)
    updated = hidden_in.astype(jnp.float32) + gate.astype(jnp.float32)[:, None, :] * projected
    return updated.astype(jnp.bfloat16)
```

```python
import functools
import math

import jax
import jax.numpy as jnp
import numpy as np
from jax import lax
from jax.experimental import pallas as pl
from jax.experimental.pallas import tpu as pltpu
from jax.sharding import Mesh, PartitionSpec as P

HEADS = 16
HD = 128
BF = jnp.bfloat16
F32 = jnp.float32
SCALE = HD**-0.5
LOG2E = math.log2(math.e)
NT = (((1,), (1,)), ((), ()))
VMEM_CAP = 56 * 2**20


def params(**kw):
    return pltpu.CompilerParams(vmem_limit_bytes=VMEM_CAP, **kw)


def pack_kernel(q_ref, k_ref, v_ref, o_ref):
    copies, heads, _, rows, _ = o_ref.shape
    for j, ref in enumerate((q_ref, k_ref, v_ref)):
        for h in range(heads):
            for r in range(copies):
                o_ref[r, h, j] = ref[r * rows : (r + 1) * rows, h * HD : (h + 1) * HD]


def pack(q, k, v, copies):
    tok, width = q.shape
    rows = tok // copies
    hb = 4
    spec = pl.BlockSpec((tok, hb * HD), lambda i: (0, i))
    return pl.pallas_call(
        pack_kernel,
        grid=(HEADS // hb,),
        in_specs=[spec] * 3,
        out_specs=pl.BlockSpec((copies, hb, 3, rows, HD), lambda i: (0, i, 0, 0, 0)),
        out_shape=jax.ShapeDtypeStruct((copies, HEADS, 3, rows, HD), BF),
        compiler_params=params(),
        name="pack",
    )(q, k, v)


def attend_kernel(*refs, first, last, groups, kb, skip_axis):
    refs = list(refs)
    q_ref = refs.pop(0)
    k_refs = [refs.pop(0) for _ in range(groups)]
    if not first:
        m_in, acc_in = refs.pop(0), refs.pop(0)
    if last:
        (o_ref,) = refs[:1]
        refs = refs[1:]
    else:
        m_out, acc_out = refs[:2]
        refs = refs[2:]
    k_all, v_all = refs
    qs = q_ref.shape[0] * q_ref.shape[2]
    total = k_all.shape[0]

    @pl.when(pl.program_id(0) == 0)
    def _():
        at = 0
        for ref in k_refs:
            n = ref.shape[0] * ref.shape[2]
            k_all[at : at + n, :] = ref[:, 0].reshape(n, HD)
            v_all[at : at + n, :HD] = ref[:, 1].reshape(n, HD)
            at += n
        v_all[:, HD:] = jnp.ones((total, HD), BF)

    q = q_ref[:, 0].reshape(qs, HD)
    c = SCALE * LOG2E
    if first:
        m = jnp.full((qs, 1), -jnp.inf, F32)
        acc = jnp.zeros((qs, 2 * HD), F32)
    else:
        m = m_in[:, :1]
        acc = acc_in[...]
    for i in range(total // kb):
        s = lax.dot_general(q, k_all[i * kb : (i + 1) * kb, :], NT, preferred_element_type=F32)
        new = jnp.maximum(m, jnp.max(s, axis=1, keepdims=True) * c)
        p = jnp.exp2(s * c - new).astype(BF)
        add = jnp.dot(p, v_all[i * kb : (i + 1) * kb, :], preferred_element_type=F32)
        if first and i == 0:
            acc = add
        else:
            acc = acc * jnp.exp2(m - new) + add
        m = new
    if last:
        out = acc[:, :HD] / acc[:, HD:]
        o_ref[...] = out.astype(BF).reshape(o_ref.shape)
    else:
        m_out[...] = jnp.broadcast_to(m, m_out.shape)
        acc_out[...] = acc


def attend(got, kv_list, state, last, qsrc=16, kb=1024):
    src, _, rows, _ = got.shape
    qb = qsrc * rows
    nq = src * rows
    total = sum(a.shape[0] * a.shape[2] for a in kv_list)
    in_specs = [pl.BlockSpec((qsrc, 1, rows, HD), lambda i: (i, 0, 0, 0))]
    args = [got]
    for a in kv_list:
        in_specs.append(pl.BlockSpec(a.shape, lambda i: (0, 0, 0, 0)))
        args.append(a)
    m_spec = pl.BlockSpec((qb, HD), lambda i: (i, 0))
    acc_spec = pl.BlockSpec((qb, 2 * HD), lambda i: (i, 0))
    if state is not None:
        in_specs += [m_spec, acc_spec]
        args += list(state)
    if last:
        out_shape = jax.ShapeDtypeStruct((src, rows, HD), BF)
        out_specs = pl.BlockSpec((qsrc, rows, HD), lambda i: (i, 0, 0))
    else:
        out_shape = (
            jax.ShapeDtypeStruct((nq, HD), F32),
            jax.ShapeDtypeStruct((nq, 2 * HD), F32),
        )
        out_specs = (m_spec, acc_spec)
    return pl.pallas_call(
        functools.partial(
            attend_kernel,
            first=state is None,
            last=last,
            groups=len(kv_list),
            kb=kb,
            skip_axis=None,
        ),
        grid=(src // qsrc,),
        in_specs=in_specs,
        out_specs=out_specs,
        out_shape=out_shape,
        scratch_shapes=[pltpu.VMEM((total, HD), BF), pltpu.VMEM((total, 2 * HD), BF)],
        compiler_params=params(),
        cost_estimate=pl.CostEstimate(
            flops=8 * nq * total * HD,
            bytes_accessed=4 * nq * HD + 4 * total * HD,
            transcendentals=nq * total,
        ),
        name="attend",
    )(*args)


def cross_kernel(q_ref, k_ref, v_ref, o_ref):
    views = k_ref.shape[0]
    heads = q_ref.shape[1] // HD
    for h in range(heads):
        cols = slice(h * HD, (h + 1) * HD)
        q = q_ref[:, cols].astype(F32)
        s = [
            jnp.sum(q * k_ref[b, :, cols].astype(F32), axis=1, keepdims=True) * SCALE
            for b in range(views)
        ]
        peak = functools.reduce(jnp.maximum, s)
        e = [jnp.exp(x - peak) for x in s]
        inv = 1.0 / functools.reduce(jnp.add, e)
        out = None
        for b in range(views):
            w = (e[b] * inv).astype(BF).astype(F32)
            t = w * v_ref[b, :, cols].astype(F32)
            out = t if out is None else out + t
        o_ref[:, cols] = out


def cross(q, k, v):
    tok, width = q.shape
    views = k.shape[0]
    hb = 4
    kv_spec = pl.BlockSpec((views, tok, hb * HD), lambda i: (0, 0, i))
    return pl.pallas_call(
        cross_kernel,
        grid=(width // (hb * HD),),
        in_specs=[pl.BlockSpec((tok, hb * HD), lambda i: (0, i)), kv_spec, kv_spec],
        out_specs=pl.BlockSpec((tok, hb * HD), lambda i: (0, i)),
        out_shape=jax.ShapeDtypeStruct((tok, width), F32),
        compiler_params=params(),
        cost_estimate=pl.CostEstimate(
            flops=16 * tok * width, bytes_accessed=(4 * views + 6) * tok * width, transcendentals=0
        ),
        name="cross",
    )(q, k, v)


def project_kernel(s_ref, c_ref, w_ref, h_ref, g_ref, o_ref, att):
    copies, heads, rows, _ = s_ref.shape

    @pl.when(pl.program_id(0) == 0)
    def _():
        for r in range(copies):
            for h in range(heads):
                at = (slice(r * rows, (r + 1) * rows), slice(h * HD, (h + 1) * HD))
                att[at] = (s_ref[r, h].astype(F32) + c_ref[at]).astype(BF)

    y = jnp.dot(att[...], w_ref[...], preferred_element_type=F32)
    o_ref[...] = (h_ref[...].astype(F32) + g_ref[...].astype(F32) * y).astype(BF)


def project(self_heads, cross_out, w, hidden, gate):
    copies, heads, rows, _ = self_heads.shape
    tok, width = cross_out.shape
    nb = 512
    return pl.pallas_call(
        project_kernel,
        grid=(width // nb,),
        in_specs=[
            pl.BlockSpec(self_heads.shape, lambda i: (0, 0, 0, 0)),
            pl.BlockSpec((tok, width), lambda i: (0, 0)),
            pl.BlockSpec((width, nb), lambda i: (0, i)),
            pl.BlockSpec((tok, nb), lambda i: (0, i)),
            pl.BlockSpec((1, nb), lambda i: (0, i)),
        ],
        out_specs=pl.BlockSpec((tok, nb), lambda i: (0, i)),
        out_shape=jax.ShapeDtypeStruct((tok, width), BF),
        scratch_shapes=[pltpu.VMEM((tok, width), BF)],
        compiler_params=params(),
        name="project",
    )(self_heads, cross_out, w, hidden, gate)


def local(hidden_in, queries, keys, values, out_weight, gate):
    hidden, q, k, v = hidden_in[0], queries[0], keys[0], values[0]
    tok, width = q.shape
    copies = lax.axis_size("y")
    seq = ("y", "z", "xh")
    view = ("xl", "c")
    rows = tok // copies
    n = copies * HEADS

    packed = pack(q, k, v, copies).reshape(n, 3 * rows, HD)
    got = lax.all_to_all(packed, seq, split_axis=0, concat_axis=0, tiled=True)
    got = got.reshape(n, 3, rows, HD)
    k_views = lax.all_gather(k, view, axis=0)
    v_views = lax.all_gather(v, view, axis=0)

    kv = got[:, 1:]
    kv_all = lax.all_gather(kv, "y", axis=0, tiled=True)
    state = None
    o = attend(got, [kv_all], state, True)
    cross_out = cross(q, k_views, v_views)
    back = lax.all_to_all(o, seq, split_axis=0, concat_axis=0, tiled=True)
    out = project(back.reshape(copies, HEADS, rows, HD), cross_out, out_weight, hidden, gate)
    return out[None]


def solution(mesh):
    devices = np.asarray(mesh.devices)
    fine = Mesh(devices.reshape(2, 2, 4, 8, 2), ("xl", "c", "y", "z", "xh"))
    spec = P(("xl", "c"), ("y", "z", "xh"), None)
    return jax.shard_map(
        local,
        mesh=fine,
        in_specs=(spec, spec, spec, spec, P(), P(("xl", "c"), None)),
        out_specs=spec,
        check_vma=False,
    )
```

```python
import functools
import math

import jax
import jax.numpy as jnp
import numpy as np
from jax import lax
from jax.experimental import pallas as pl
from jax.experimental.pallas import tpu as pltpu
from jax.sharding import Mesh, PartitionSpec as P

HEADS = 16
HD = 128
BF = jnp.bfloat16
F32 = jnp.float32
SCALE = HD**-0.5
LOG2E = math.log2(math.e)
NT = (((1,), (1,)), ((), ()))
VMEM_CAP = 30 * 2**20


def params(**kw):
    return pltpu.CompilerParams(vmem_limit_bytes=VMEM_CAP, **kw)


def pack_kernel(q_ref, k_ref, v_ref, o_ref):
    copies, heads, _, rows, _ = o_ref.shape
    for j, ref in enumerate((q_ref, k_ref, v_ref)):
        for h in range(heads):
            for r in range(copies):
                o_ref[r, h, j] = ref[r * rows : (r + 1) * rows, h * HD : (h + 1) * HD]


def pack(q, k, v, copies):
    tok, width = q.shape
    rows = tok // copies
    hb = 4
    spec = pl.BlockSpec((tok, hb * HD), lambda i: (0, i))
    return pl.pallas_call(
        pack_kernel,
        grid=(HEADS // hb,),
        in_specs=[spec] * 3,
        out_specs=pl.BlockSpec((copies, hb, 3, rows, HD), lambda i: (0, i, 0, 0, 0)),
        out_shape=jax.ShapeDtypeStruct((copies, HEADS, 3, rows, HD), BF),
        compiler_params=params(),
        name="pack",
    )(q, k, v)


def attend_kernel(*refs, first, last, groups, kb):
    refs = list(refs)
    q_ref = refs.pop(0)
    k_refs = [refs.pop(0) for _ in range(groups)]
    if not first:
        m_in, acc_in = refs.pop(0), refs.pop(0)
    if last:
        (o_ref,) = refs[:1]
        refs = refs[1:]
    else:
        m_out, acc_out = refs[:2]
        refs = refs[2:]
    k_all, v_all = refs
    qs = q_ref.shape[0] * q_ref.shape[2]
    total = k_all.shape[0]

    @pl.when(pl.program_id(0) == 0)
    def _():
        at = 0
        for ref in k_refs:
            n = ref.shape[0] * ref.shape[2]
            k_all[at : at + n, :] = ref[:, 0].reshape(n, HD)
            v_all[at : at + n, :HD] = ref[:, 1].reshape(n, HD)
            at += n
        v_all[:, HD:] = jnp.ones((total, HD), BF)

    q = q_ref[:, 0].reshape(qs, HD)
    c = SCALE * LOG2E
    if first:
        m = jnp.full((qs, 1), -jnp.inf, F32)
        acc = jnp.zeros((qs, 2 * HD), F32)
    else:
        m = m_in[:, :1]
        acc = acc_in[...]
    for i in range(total // kb):
        s = lax.dot_general(q, k_all[i * kb : (i + 1) * kb, :], NT, preferred_element_type=F32)
        new = jnp.maximum(m, jnp.max(s, axis=1, keepdims=True) * c)
        p = jnp.exp2(s * c - new).astype(BF)
        add = jnp.dot(p, v_all[i * kb : (i + 1) * kb, :], preferred_element_type=F32)
        if first and i == 0:
            acc = add
        else:
            acc = acc * jnp.exp2(m - new) + add
        m = new
    if last:
        out = acc[:, :HD] / acc[:, HD:]
        o_ref[...] = out.astype(BF).reshape(o_ref.shape)
    else:
        m_out[...] = jnp.broadcast_to(m, m_out.shape)
        acc_out[...] = acc


def attend(got, kv_list, state, last, qsrc=16, kb=1024):
    src, _, rows, _ = got.shape
    qb = qsrc * rows
    nq = src * rows
    total = sum(a.shape[0] * a.shape[2] for a in kv_list)
    in_specs = [pl.BlockSpec((qsrc, 1, rows, HD), lambda i: (i, 0, 0, 0))]
    args = [got]
    for a in kv_list:
        in_specs.append(pl.BlockSpec(a.shape, lambda i: (0, 0, 0, 0)))
        args.append(a)
    m_spec = pl.BlockSpec((qb, HD), lambda i: (i, 0))
    acc_spec = pl.BlockSpec((qb, 2 * HD), lambda i: (i, 0))
    if state is not None:
        in_specs += [m_spec, acc_spec]
        args += list(state)
    if last:
        out_shape = jax.ShapeDtypeStruct((src, rows, HD), BF)
        out_specs = pl.BlockSpec((qsrc, rows, HD), lambda i: (i, 0, 0))
    else:
        out_shape = (
            jax.ShapeDtypeStruct((nq, HD), F32),
            jax.ShapeDtypeStruct((nq, 2 * HD), F32),
        )
        out_specs = (m_spec, acc_spec)
    return pl.pallas_call(
        functools.partial(
            attend_kernel,
            first=state is None,
            last=last,
            groups=len(kv_list),
            kb=kb,
        ),
        grid=(src // qsrc,),
        in_specs=in_specs,
        out_specs=out_specs,
        out_shape=out_shape,
        scratch_shapes=[pltpu.VMEM((total, HD), BF), pltpu.VMEM((total, 2 * HD), BF)],
        compiler_params=params(),
        cost_estimate=pl.CostEstimate(
            flops=8 * nq * total * HD,
            bytes_accessed=4 * nq * HD + 4 * total * HD,
            transcendentals=nq * total,
        ),
        name="attend",
    )(*args)


def cross_kernel(a_ref, b_ref, o_ref):
    views, parts, heads = a_ref.shape[:3]
    for r in range(parts):
        for h in range(heads):
            ks = [a_ref[b, r, h, 1].astype(F32) for b in range(views)]
            ks += [b_ref[b, r, h, 0].astype(F32) for b in range(views)]
            vs = [a_ref[b, r, h, 2].astype(F32) for b in range(views)]
            vs += [b_ref[b, r, h, 1].astype(F32) for b in range(views)]
            for a in range(views):
                q = a_ref[a, r, h, 0].astype(F32)
                s = [jnp.sum(q * k, axis=1, keepdims=True) * SCALE for k in ks]
                peak = functools.reduce(jnp.maximum, s)
                e = [jnp.exp(x - peak) for x in s]
                inv = 1.0 / functools.reduce(jnp.add, e)
                terms = [(x * inv).astype(BF).astype(F32) * v for x, v in zip(e, vs)]
                o_ref[a, r, h] = functools.reduce(jnp.add, terms)


def cross(mine, other):
    views, parts, heads, _, rows, _ = mine.shape
    hb = 4
    size = views * parts * heads * rows * HD
    return pl.pallas_call(
        cross_kernel,
        grid=(heads // hb,),
        in_specs=[
            pl.BlockSpec((views, parts, hb, 3, rows, HD), lambda i: (0, 0, i, 0, 0, 0)),
            pl.BlockSpec((views, parts, hb, 2, rows, HD), lambda i: (0, 0, i, 0, 0, 0)),
        ],
        out_specs=pl.BlockSpec((views, parts, hb, rows, HD), lambda i: (0, 0, i, 0, 0)),
        out_shape=jax.ShapeDtypeStruct((views, parts, heads, rows, HD), F32),
        compiler_params=params(),
        cost_estimate=pl.CostEstimate(
            flops=16 * size, bytes_accessed=14 * size, transcendentals=0
        ),
        name="cross",
    )(mine, other)


def project_kernel(a_ref, w_ref, h_ref, g_ref, o_ref, att):
    copies, heads, rows, _ = a_ref.shape

    @pl.when(pl.program_id(0) == 0)
    def _():
        for r in range(copies):
            for h in range(heads):
                att[r * rows : (r + 1) * rows, h * HD : (h + 1) * HD] = a_ref[r, h]

    y = jnp.dot(att[...], w_ref[...], preferred_element_type=F32)
    o_ref[...] = (h_ref[...].astype(F32) + g_ref[...].astype(F32) * y).astype(BF)


def project(attended, w, hidden, gate):
    copies, heads, rows, _ = attended.shape
    tok, width = hidden.shape
    nb = 512
    return pl.pallas_call(
        project_kernel,
        grid=(width // nb,),
        in_specs=[
            pl.BlockSpec(attended.shape, lambda i: (0, 0, 0, 0)),
            pl.BlockSpec((width, nb), lambda i: (0, i)),
            pl.BlockSpec((tok, nb), lambda i: (0, i)),
            pl.BlockSpec((1, nb), lambda i: (0, i)),
        ],
        out_specs=pl.BlockSpec((tok, nb), lambda i: (0, i)),
        out_shape=jax.ShapeDtypeStruct((tok, width), BF),
        scratch_shapes=[pltpu.VMEM((tok, width), BF)],
        compiler_params=params(),
        name="project",
    )(attended, w, hidden, gate)


SWAP = [(0, 1), (1, 0)]
CHUNKS = 4


def swap(chunks, axis):
    return [lax.ppermute(x, axis, SWAP) for x in chunks]


def local(hidden_in, queries, keys, values, out_weight, gate):
    hidden, q, k, v = hidden_in[0], queries[0], keys[0], values[0]
    tok, _ = q.shape
    seq = ("yv", "yr", "z", "xh")
    rows = tok // 4
    n = 4 * HEADS

    packed = pack(q, k, v, 4)
    mine = lax.all_to_all(packed, "c", split_axis=0, concat_axis=0, tiled=True)
    mine = mine.reshape(2, 2, HEADS, 3, rows, HD)
    got = lax.all_to_all(mine.reshape(n, 3 * rows, HD), seq, split_axis=0, concat_axis=0, tiled=True)
    got = got.reshape(n, 3, rows, HD)

    step = n // CHUNKS
    own = [got[i * step : (i + 1) * step, 1:] for i in range(CHUNKS)]
    mate = swap([got[: n // 2, 1:], got[n // 2 :, 1:]], "yr")
    other = lax.ppermute(mine[:, :, :, 1:], "xl", SWAP)
    own_pair = swap(own, "c")
    state = attend(got, own + own_pair, None, False)
    mate, other, state = lax.optimization_barrier((mate, other, state))
    cross_out = cross(mine, other)
    mate_pair = swap([x[i * step : (i + 1) * step] for x in mate for i in range(2)], "c")
    cross_out, state = lax.optimization_barrier((cross_out, state))
    o = attend(got, mate + mate_pair, state, True)

    back = lax.all_to_all(o, seq, split_axis=0, concat_axis=0, tiled=True)
    attended = (back.reshape(cross_out.shape).astype(F32) + cross_out).astype(BF)
    attended = lax.all_to_all(
        attended.reshape(4, HEADS, rows, HD), "c", split_axis=0, concat_axis=0, tiled=True
    )
    return project(attended, out_weight, hidden, gate)[None]


def solution(mesh):
    devices = np.asarray(mesh.devices)
    fine = Mesh(devices.reshape(2, 2, 2, 2, 8, 2), ("xl", "c", "yv", "yr", "z", "xh"))
    view, seq = ("xl", "c"), ("yv", "yr", "z", "xh")
    spec = P(view, seq, None)
    return jax.shard_map(
        local,
        mesh=fine,
        in_specs=(spec, spec, spec, spec, P(), P(view, None)),
        out_specs=spec,
        check_vma=False,
    )
```

```python
import functools
import math

import jax
import jax.numpy as jnp
import numpy as np
from jax import lax
from jax.experimental import pallas as pl
from jax.experimental.pallas import tpu as pltpu
from jax.sharding import Mesh, PartitionSpec as P

HEADS = 16
HD = 128
BF = jnp.bfloat16
F32 = jnp.float32
SCALE = HD**-0.5
LOG2E = math.log2(math.e)
NT = (((1,), (1,)), ((), ()))
VMEM_CAP = 30 * 2**20


def params(**kw):
    return pltpu.CompilerParams(vmem_limit_bytes=VMEM_CAP, **kw)


def whole(n):
    return [pl.BlockSpec(memory_space=pltpu.VMEM)] * n


def pack_kernel(q_ref, k_ref, v_ref, o_ref, sq_ref, sk_ref, sv_ref, held, sems):
    _, parts, heads, _, rows, _ = o_ref.shape
    half = parts * rows
    me = lax.axis_index("c")
    moves = []
    for to, core in ((0, 1 - me), (1, me)):
        for j, ref in enumerate((q_ref, k_ref, v_ref)):
            part = pl.ds(pl.multiple_of(core * half, half), half)
            moves.append(pltpu.make_async_copy(ref.at[part], held.at[to, j], sems.at[to, j]))
    for move in moves:
        move.start()
    for j, out in enumerate((sq_ref, sk_ref, sv_ref)):
        moves[j].wait()
        for r in range(parts):
            for h in range(heads):
                out[r, h] = held[0, j, r * rows : (r + 1) * rows, h * HD : (h + 1) * HD]
    for j in range(3):
        moves[3 + j].wait()
        for r in range(parts):
            for h in range(heads):
                o_ref[me, r, h, j] = held[1, j, r * rows : (r + 1) * rows, h * HD : (h + 1) * HD]


def pack(q, k, v):
    tok, width = q.shape
    rows = tok // 4
    away = jax.ShapeDtypeStruct((2, HEADS, rows, HD), BF)
    return pl.pallas_call(
        pack_kernel,
        in_specs=[pl.BlockSpec(memory_space=pltpu.HBM)] * 3,
        out_specs=whole(4),
        out_shape=[jax.ShapeDtypeStruct((2, 2, HEADS, 3, rows, HD), BF)] + [away] * 3,
        scratch_shapes=[
            pltpu.VMEM((2, 3, tok // 2, width), BF),
            pltpu.SemaphoreType.DMA((2, 3)),
        ],
        compiler_params=params(),
        name="pack",
    )(*(pltpu.with_memory_space_constraint(x, pltpu.HBM) for x in (q, k, v)))


def place_kernel(a_ref, q_ref, k_ref, v_ref, o_ref):
    _, parts, heads = a_ref.shape[:3]
    you = 1 - lax.axis_index("c")
    for j, ref in enumerate((q_ref, k_ref, v_ref)):
        for r in range(parts):
            for h in range(heads):
                o_ref[you, r, h, j] = ref[r, h]


def place(mine, got):
    return pl.pallas_call(
        place_kernel,
        in_specs=whole(4),
        out_specs=pl.BlockSpec(memory_space=pltpu.VMEM),
        out_shape=jax.ShapeDtypeStruct(mine.shape, BF),
        input_output_aliases={0: 0},
        compiler_params=params(),
        name="place",
    )(mine, *got)


def gather_kv(kv_refs, k_all, v_all):
    at = 0
    for ref in kv_refs:
        n = ref.shape[0] * ref.shape[2]
        k_all[at : at + n, :] = ref[:, 0].reshape(n, HD)
        v_all[at : at + n, :HD] = ref[:, 1].reshape(n, HD)
        at += n
    v_all[:, HD:] = jnp.ones((at, HD), BF)


def eye():
    shape = (HD, HD)
    return lax.broadcasted_iota(jnp.int32, shape, 0) == lax.broadcasted_iota(jnp.int32, shape, 1)


def attend_block(q, k_all, v_all, kb):
    c = SCALE * LOG2E
    total = k_all.shape[0]

    def score(i):
        return lax.dot_general(q, k_all[i * kb : (i + 1) * kb, :], NT, preferred_element_type=F32)

    m = acc = None
    s = score(0)
    for i in range(total // kb):
        following = score(i + 1) if (i + 1) * kb < total else None
        peak = jnp.max(s, axis=1, keepdims=True) * c
        new = peak if m is None else jnp.maximum(m, peak)
        p = jnp.exp2(s * c - new).astype(BF)
        add = jnp.dot(p, v_all[i * kb : (i + 1) * kb, :], preferred_element_type=F32)
        acc = add if acc is None else acc * jnp.exp2(m - new) + add
        m, s = new, following
    return acc[:, :HD] / acc[:, HD:], m + jnp.log2(acc[:, HD:])


def attend_kernel(*refs, first, travels, qb, kb):
    if first:
        q_ref, *kv_refs, o_ref, l_ref, k_all, v_all = refs
        gather_kv(kv_refs, k_all, v_all)
    else:
        q_ref, k_all, v_all, o_ref, l_ref = refs
    src, rows, _ = q_ref.shape
    qsrc = qb // rows
    diag = eye()
    for j in range(src // qsrc):
        q = q_ref[j * qsrc : (j + 1) * qsrc].reshape(qb, HD)
        o, lse = attend_block(q, k_all, v_all, kb)
        o_ref[j * qsrc : (j + 1) * qsrc] = o.reshape(qsrc, rows, HD).astype(o_ref.dtype)
        for g in range(qb // HD):
            line = jnp.where(diag, lse[g * HD : (g + 1) * HD], 0.0)
            l_ref[j * (qb // HD) + g, :] = jnp.sum(line, axis=0)
    if travels:
        lines = l_ref.shape[0]
        lse = l_ref[...]
        terms = []
        for _ in range(3):
            terms.append(lse.astype(BF))
            lse = lse - terms[-1].astype(F32)
        terms.append(jnp.zeros((rows - 3 * lines, HD), BF))
        o_ref[src] = jnp.concatenate(terms, axis=0)


def attend(q, kv, first, travels, qb=512, kb=2048):
    src, rows, _ = q.shape
    nq = src * rows
    total = sum(a.shape[0] * a.shape[2] for a in kv) if first else kv[0].shape[0]
    out_shape = [
        jax.ShapeDtypeStruct((src + travels, rows, HD), BF if travels else F32),
        jax.ShapeDtypeStruct((nq // HD, HD), F32),
    ]
    if first:
        out_shape += [
            jax.ShapeDtypeStruct((total, HD), BF),
            jax.ShapeDtypeStruct((total, 2 * HD), BF),
        ]
    return pl.pallas_call(
        functools.partial(attend_kernel, first=first, travels=travels, qb=qb, kb=min(kb, total)),
        in_specs=whole(1 + len(kv)),
        out_specs=whole(len(out_shape)),
        out_shape=out_shape,
        compiler_params=params(),
        cost_estimate=pl.CostEstimate(
            flops=0,
            bytes_accessed=0,
            transcendentals=0,
        ),
        name="attend",
    )(q, *kv)


def merge_kernel(*refs):
    *parts, out_ref = refs
    diag = eye()
    at = 0
    while parts:
        oa, la, ob = parts[:3]
        parts = parts[3:]
        src, rows, _ = oa.shape
        lines, per = la.shape[0], HD // rows
        terms = ob[src].astype(F32)
        lb = terms[:lines] + terms[lines : 2 * lines] + terms[2 * lines : 3 * lines]
        peak = jnp.maximum(la[...], lb)
        ea, eb = jnp.exp2(la[...] - peak), jnp.exp2(lb - peak)
        wa = ea / (ea + eb)
        for g in range(lines):
            w = jnp.sum(jnp.where(diag, wa[g : g + 1, :], 0.0), axis=1, keepdims=True)
            a = oa[g * per : (g + 1) * per].reshape(HD, HD)
            b = ob[g * per : (g + 1) * per].reshape(HD, HD).astype(F32)
            out = (b + w * (a - b)).astype(BF)
            out_ref[at + g * per : at + (g + 1) * per] = out.reshape(per, rows, HD)
        at += src


def merge(parts):
    src = sum(p[0].shape[0] for p in parts)
    flat = [x for p in parts for x in p]
    return pl.pallas_call(
        merge_kernel,
        in_specs=whole(len(flat)),
        out_specs=pl.BlockSpec(memory_space=pltpu.VMEM),
        out_shape=jax.ShapeDtypeStruct((src,) + parts[0][0].shape[1:], BF),
        compiler_params=params(),
        name="merge",
    )(*flat)


def cross_kernel(a_ref, b_ref, o_ref):
    views, parts, heads = a_ref.shape[:3]

    def one_head(h, carry):
        for r in range(parts):
            ks = [a_ref[b, r, h, 1].astype(F32) for b in range(views)]
            ks += [b_ref[b, r, h, 0].astype(F32) for b in range(views)]
            vs = [a_ref[b, r, h, 2].astype(F32) for b in range(views)]
            vs += [b_ref[b, r, h, 1].astype(F32) for b in range(views)]
            for a in range(views):
                q = a_ref[a, r, h, 0].astype(F32)
                s = [jnp.sum(q * k, axis=1, keepdims=True) * SCALE for k in ks]
                peak = functools.reduce(jnp.maximum, s)
                e = [jnp.exp(x - peak) for x in s]
                inv = 1.0 / functools.reduce(jnp.add, e)
                terms = [(x * inv).astype(BF).astype(F32) * v for x, v in zip(e, vs)]
                o_ref[a, r, h] = functools.reduce(jnp.add, terms)
        return carry

    lax.fori_loop(0, heads, one_head, 0)


def cross(mine, other):
    views, parts, heads, _, rows, _ = mine.shape
    return pl.pallas_call(
        cross_kernel,
        in_specs=whole(2),
        out_specs=pl.BlockSpec(memory_space=pltpu.VMEM),
        out_shape=jax.ShapeDtypeStruct((views, parts, heads, rows, HD), F32),
        compiler_params=params(),
        name="cross",
    )(mine, other)


def add_kernel(s_ref, c_ref, keep_ref, send_ref):
    me = lax.axis_index("c")
    for view, out in ((1 - me, send_ref), (me, keep_ref)):
        out[...] = (s_ref[view].astype(F32) + c_ref[view]).astype(BF)


def add_cross(self_out, cross_out):
    out = jax.ShapeDtypeStruct(self_out.shape[1:], BF)
    return pl.pallas_call(
        add_kernel,
        in_specs=whole(2),
        out_specs=whole(2),
        out_shape=[out, out],
        compiler_params=params(),
        name="add_cross",
    )(self_out, cross_out)


def project_kernel(keep_ref, came_ref, w_ref, h_ref, g_ref, o_ref, att):
    half = o_ref.shape[0] // 2
    me = lax.axis_index("c")
    for core, ref in ((me, keep_ref), (1 - me, came_ref)):
        parts, heads, rows, _ = ref.shape
        for r in range(parts):
            at = pl.ds(pl.multiple_of(core * half + r * rows, rows), rows)
            for h in range(heads):
                att[at, h * HD : (h + 1) * HD] = ref[r, h]
    nb = 512
    for i in range(o_ref.shape[1] // nb):
        cols = slice(i * nb, (i + 1) * nb)
        y = jnp.dot(att[...], w_ref[:, cols], preferred_element_type=F32)
        o_ref[:, cols] = (h_ref[:, cols].astype(F32) + g_ref[:, cols].astype(F32) * y).astype(BF)


def project(keep, came, w, hidden, gate):
    return pl.pallas_call(
        project_kernel,
        in_specs=whole(5),
        out_specs=pl.BlockSpec(memory_space=pltpu.VMEM),
        out_shape=jax.ShapeDtypeStruct(hidden.shape, BF),
        scratch_shapes=[pltpu.VMEM(hidden.shape, BF)],
        compiler_params=params(),
        name="project",
    )(keep, came, w, hidden, gate)


SWAP = [(0, 1), (1, 0)]
CHUNKS = 4


def swap(chunks, axis):
    return [lax.ppermute(x, axis, SWAP) for x in chunks]


def local(hidden_in, queries, keys, values, out_weight, gate):
    hidden, q, k, v = hidden_in[0], queries[0], keys[0], values[0]
    tok, _ = q.shape
    seq = ("yv", "yr", "z", "xh")
    rows = tok // 4
    n = 4 * HEADS

    mine, *away = pack(q, k, v)
    mine = place(mine, swap(away, "c"))
    got = lax.all_to_all(mine.reshape(n, 3 * rows, HD), seq, split_axis=0, concat_axis=0, tiled=True)
    got = got.reshape(n, 3, rows, HD)

    step, half = n // CHUNKS, n // 2
    own = [got[i * step : (i + 1) * step, 1:] for i in range(CHUNKS)]
    own_pair = swap(own, "c")
    qs = [got[:half, 0], got[half:, 0]]
    mate_q = swap(qs, "yr")

    o1, l1, keys_all, values_all = attend(qs[0], own + own_pair, True, False)
    kv = keys_all, values_all
    q_in, away, o1 = lax.optimization_barrier((mate_q[0], mine, o1))
    other = lax.ppermute(away[:, :, :, 1:], "xl", SWAP)
    mo1, _ = attend(q_in, kv, False, True)
    back1 = lax.ppermute(mo1, "yr", SWAP)
    q_in, mo1 = lax.optimization_barrier((mate_q[1], mo1))
    mo2, _ = attend(q_in, kv, False, True)
    back2 = lax.ppermute(mo2, "yr", SWAP)
    q_in, back1, mo2 = lax.optimization_barrier((qs[1], back1, mo2))
    o2, l2 = attend(q_in, kv, False, False)
    o = merge([(o1, l1, back1), (o2, l2, back2)])
    back = lax.all_to_all(o, seq, split_axis=0, concat_axis=0, tiled=True)
    here, back = lax.optimization_barrier((mine, back))
    cross_out = cross(here, other)
    keep, send = add_cross(back.reshape(cross_out.shape), cross_out)
    came = lax.ppermute(send, "c", SWAP)
    return project(keep, came, out_weight, hidden, gate)[None]


def solution(mesh):
    devices = np.asarray(mesh.devices)
    fine = Mesh(devices.reshape(2, 2, 2, 2, 8, 2), ("xl", "c", "yv", "yr", "z", "xh"))
    view, seq = ("xl", "c"), ("yv", "yr", "z", "xh")
    spec = P(view, seq, None)
    return jax.shard_map(
        local,
        mesh=fine,
        in_specs=(spec, spec, spec, spec, P(), P(view, None)),
        out_specs=spec,
        check_vma=False,
    )
```

```python
import functools
import math

import jax
import jax.numpy as jnp
import numpy as np
from jax import lax
from jax.experimental import pallas as pl
from jax.experimental.pallas import tpu as pltpu
from jax.sharding import Mesh, PartitionSpec as P

HEADS = 16
HD = 128
BF = jnp.bfloat16
F32 = jnp.float32
SCALE = HD**-0.5
LOG2E = math.log2(math.e)
NT = (((1,), (1,)), ((), ()))
VMEM_CAP = 30 * 2**20


def params(**kw):
    return pltpu.CompilerParams(vmem_limit_bytes=VMEM_CAP, **kw)


def whole(n):
    return [pl.BlockSpec(memory_space=pltpu.VMEM)] * n


def fetch_half(core, refs, held, sems):
    half = held.shape[1]
    part = pl.ds(pl.multiple_of(core * half, half), half)
    moves = [
        pltpu.make_async_copy(ref.at[part], held.at[j], sems.at[j]) for j, ref in enumerate(refs)
    ]
    for move in moves:
        move.start()
    return moves


def pack_send_kernel(q_ref, k_ref, v_ref, sq_ref, sk_ref, sv_ref, held, sems):
    moves = fetch_half(1 - lax.axis_index("c"), (q_ref, k_ref, v_ref), held, sems)
    for j, out in enumerate((sq_ref, sk_ref, sv_ref)):
        moves[j].wait()
        for h in range(out.shape[1]):
            out[0, h] = held[j, :, h * HD : (h + 1) * HD]


def pack_keep_kernel(q_ref, k_ref, v_ref, o_ref, held, sems):
    me = lax.axis_index("c")
    moves = fetch_half(me, (q_ref, k_ref, v_ref), held, sems)
    for j in range(3):
        moves[j].wait()
        for h in range(o_ref.shape[2]):
            o_ref[me, 0, h, j] = held[j, :, h * HD : (h + 1) * HD]


def pack(kernel, out_shape, q, k, v):
    tok, width = q.shape
    return pl.pallas_call(
        kernel,
        in_specs=[pl.BlockSpec(memory_space=pltpu.HBM)] * 3,
        out_specs=whole(len(out_shape)),
        out_shape=[jax.ShapeDtypeStruct(x, BF) for x in out_shape],
        scratch_shapes=[pltpu.VMEM((3, tok // 2, width), BF), pltpu.SemaphoreType.DMA((3,))],
        compiler_params=params(),
        name="pack",
    )(*(pltpu.with_memory_space_constraint(x, pltpu.HBM) for x in (q, k, v)))


def place_kernel(a_ref, q_ref, k_ref, v_ref, o_ref):
    _, parts, heads = a_ref.shape[:3]
    you = 1 - lax.axis_index("c")
    for j, ref in enumerate((q_ref, k_ref, v_ref)):
        for r in range(parts):
            for h in range(heads):
                o_ref[you, r, h, j] = ref[r, h]


def place(mine, got):
    return pl.pallas_call(
        place_kernel,
        in_specs=whole(4),
        out_specs=pl.BlockSpec(memory_space=pltpu.VMEM),
        out_shape=jax.ShapeDtypeStruct(mine.shape, BF),
        input_output_aliases={0: 0},
        compiler_params=params(),
        name="place",
    )(mine, *got)


def gather_kv(kv_refs, k_all, v_all):
    at = 0
    for ref in kv_refs:
        n = ref.shape[0] * ref.shape[2]
        k_all[at : at + n, :] = ref[:, 0].reshape(n, HD)
        v_all[at : at + n, :HD] = ref[:, 1].reshape(n, HD)
        at += n
    v_all[:, HD:] = jnp.ones((at, HD), BF)


def eye():
    shape = (HD, HD)
    return lax.broadcasted_iota(jnp.int32, shape, 0) == lax.broadcasted_iota(jnp.int32, shape, 1)


def attend_block(q, k_all, v_all, kb):
    c = SCALE * LOG2E
    total = k_all.shape[0]

    def score(i):
        return lax.dot_general(q, k_all[i * kb : (i + 1) * kb, :], NT, preferred_element_type=F32)

    m = acc = None
    s = score(0)
    for i in range(total // kb):
        following = score(i + 1) if (i + 1) * kb < total else None
        peak = jnp.max(s, axis=1, keepdims=True) * c
        new = peak if m is None else jnp.maximum(m, peak)
        p = jnp.exp2(s * c - new).astype(BF)
        add = jnp.dot(p, v_all[i * kb : (i + 1) * kb, :], preferred_element_type=F32)
        acc = add if acc is None else acc * jnp.exp2(m - new) + add
        m, s = new, following
    return acc[:, :HD] / acc[:, HD:], m + jnp.log2(acc[:, HD:])


def attend_kernel(*refs, first, travels, qb, kb):
    if first:
        q_ref, *kv_refs, o_ref, l_ref, k_all, v_all = refs
        gather_kv(kv_refs, k_all, v_all)
    else:
        q_ref, k_all, v_all, o_ref, l_ref = refs
    src, rows, _ = q_ref.shape
    qsrc = qb // rows
    diag = eye()
    for j in range(src // qsrc):
        q = q_ref[j * qsrc : (j + 1) * qsrc].reshape(qb, HD)
        o, lse = attend_block(q, k_all, v_all, kb)
        o_ref[j * qsrc : (j + 1) * qsrc] = o.reshape(qsrc, rows, HD).astype(o_ref.dtype)
        for g in range(qb // HD):
            line = jnp.where(diag, lse[g * HD : (g + 1) * HD], 0.0)
            l_ref[j * (qb // HD) + g, :] = jnp.sum(line, axis=0)
    if travels:
        lines = l_ref.shape[0]
        lse = l_ref[...]
        terms = []
        for _ in range(3):
            terms.append(lse.astype(BF))
            lse = lse - terms[-1].astype(F32)
        terms.append(jnp.zeros((rows - 3 * lines, HD), BF))
        o_ref[src] = jnp.concatenate(terms, axis=0)


def attend(q, kv, first, travels, qb=512, kb=2048):
    src, rows, _ = q.shape
    nq = src * rows
    total = sum(a.shape[0] * a.shape[2] for a in kv) if first else kv[0].shape[0]
    out_shape = [
        jax.ShapeDtypeStruct((src + travels, rows, HD), BF if travels else F32),
        jax.ShapeDtypeStruct((nq // HD, HD), F32),
    ]
    if first:
        out_shape += [
            jax.ShapeDtypeStruct((total, HD), BF),
            jax.ShapeDtypeStruct((total, 2 * HD), BF),
        ]
    return pl.pallas_call(
        functools.partial(attend_kernel, first=first, travels=travels, qb=qb, kb=min(kb, total)),
        in_specs=whole(1 + len(kv)),
        out_specs=whole(len(out_shape)),
        out_shape=out_shape,
        compiler_params=params(),
        cost_estimate=pl.CostEstimate(
            flops=0,
            bytes_accessed=0,
            transcendentals=0,
        ),
        name="attend",
    )(q, *kv)


def merge_kernel(*refs):
    *parts, out_ref = refs
    diag = eye()
    at = 0
    while parts:
        oa, la, ob = parts[:3]
        parts = parts[3:]
        src, rows, _ = oa.shape
        lines, per = la.shape[0], HD // rows
        terms = ob[src].astype(F32)
        lb = terms[:lines] + terms[lines : 2 * lines] + terms[2 * lines : 3 * lines]
        peak = jnp.maximum(la[...], lb)
        ea, eb = jnp.exp2(la[...] - peak), jnp.exp2(lb - peak)
        wa = ea / (ea + eb)
        for g in range(lines):
            w = jnp.sum(jnp.where(diag, wa[g : g + 1, :], 0.0), axis=1, keepdims=True)
            a = oa[g * per : (g + 1) * per].reshape(HD, HD)
            b = ob[g * per : (g + 1) * per].reshape(HD, HD).astype(F32)
            out = (b + w * (a - b)).astype(BF)
            out_ref[at + g * per : at + (g + 1) * per] = out.reshape(per, rows, HD)
        at += src


def merge(parts):
    src = sum(p[0].shape[0] for p in parts)
    flat = [x for p in parts for x in p]
    return pl.pallas_call(
        merge_kernel,
        in_specs=whole(len(flat)),
        out_specs=pl.BlockSpec(memory_space=pltpu.VMEM),
        out_shape=jax.ShapeDtypeStruct((src,) + parts[0][0].shape[1:], BF),
        compiler_params=params(),
        name="merge",
    )(*flat)


def cross_kernel(a_ref, b_ref, s_ref, o_ref, *, flip):
    views, parts, heads = a_ref.shape[:3]
    view = lax.axis_index("c")
    if flip:
        view = 1 - view

    def one_head(h, carry):
        for r in range(parts):
            ks = [a_ref[b, r, h, 1].astype(F32) for b in range(views)]
            ks += [b_ref[b, r, h, 0].astype(F32) for b in range(views)]
            vs = [a_ref[b, r, h, 2].astype(F32) for b in range(views)]
            vs += [b_ref[b, r, h, 1].astype(F32) for b in range(views)]
            q = a_ref[view, r, h, 0].astype(F32)
            s = [jnp.sum(q * k, axis=1, keepdims=True) * SCALE for k in ks]
            peak = functools.reduce(jnp.maximum, s)
            e = [jnp.exp(x - peak) for x in s]
            inv = 1.0 / functools.reduce(jnp.add, e)
            terms = [(x * inv).astype(BF).astype(F32) * v for x, v in zip(e, vs)]
            cross_out = functools.reduce(jnp.add, terms)
            o_ref[r, h] = (s_ref[view, r, h].astype(F32) + cross_out).astype(BF)
        return carry

    lax.fori_loop(0, heads, one_head, 0, unroll=2)


def attended(mine, other, back, flip):
    return pl.pallas_call(
        functools.partial(cross_kernel, flip=flip),
        in_specs=whole(3),
        out_specs=pl.BlockSpec(memory_space=pltpu.VMEM),
        out_shape=jax.ShapeDtypeStruct(back.shape[1:], BF),
        compiler_params=params(),
        name="cross",
    )(mine, other, back)


def project_kernel(keep_ref, came_ref, w_ref, h_ref, g_ref, o_ref, att):
    half = o_ref.shape[0] // 2
    me = lax.axis_index("c")
    for core, ref in ((me, keep_ref), (1 - me, came_ref)):
        parts, heads, rows, _ = ref.shape
        for r in range(parts):
            at = pl.ds(pl.multiple_of(core * half + r * rows, rows), rows)
            for h in range(heads):
                att[at, h * HD : (h + 1) * HD] = ref[r, h]
    nb = 512
    for i in range(o_ref.shape[1] // nb):
        cols = slice(i * nb, (i + 1) * nb)
        y = jnp.dot(att[...], w_ref[:, cols], preferred_element_type=F32)
        o_ref[:, cols] = (h_ref[:, cols].astype(F32) + g_ref[:, cols].astype(F32) * y).astype(BF)


def project(keep, came, w, hidden, gate):
    return pl.pallas_call(
        project_kernel,
        in_specs=whole(5),
        out_specs=pl.BlockSpec(memory_space=pltpu.VMEM),
        out_shape=jax.ShapeDtypeStruct(hidden.shape, BF),
        scratch_shapes=[pltpu.VMEM(hidden.shape, BF)],
        compiler_params=params(),
        name="project",
    )(keep, came, w, hidden, gate)


SWAP = [(0, 1), (1, 0)]
CHUNKS = 4


def swap(chunks, axis):
    return [lax.ppermute(x, axis, SWAP) for x in chunks]


def local(hidden_in, queries, keys, values, out_weight, gate):
    hidden, q, k, v = hidden_in[0], queries[0], keys[0], values[0]
    tok, _ = q.shape
    seq = ("yv", "z", "xh")
    rows = tok // 2
    n = 2 * HEADS

    away = pack(pack_send_kernel, [(1, HEADS, rows, HD)] * 3, q, k, v)
    came = swap(away, "c")
    (mine,) = pack(pack_keep_kernel, [(2, 1, HEADS, 3, rows, HD)], q, k, v)
    mine = place(mine, came)
    got = lax.all_to_all(mine.reshape(n, 3 * rows, HD), seq, split_axis=0, concat_axis=0, tiled=True)
    got = got.reshape(n, 3, rows, HD)

    step, half = n // CHUNKS, n // 2
    own = [got[i * step : (i + 1) * step, 1:] for i in range(CHUNKS)]
    own_pair = swap(own, "c")
    qs = [got[:half, 0], got[half:, 0]]
    mate_q = swap(qs, "yr")

    o1, l1, keys_all, values_all = attend(qs[0], own + own_pair, True, False)
    kv = keys_all, values_all
    q_in, away, o1 = lax.optimization_barrier((mate_q[0], mine, o1))
    other = lax.ppermute(away[:, :, :, 1:], "xl", SWAP)
    mo1, _ = attend(q_in, kv, False, True)
    back1 = lax.ppermute(mo1, "yr", SWAP)
    q_in, mo1 = lax.optimization_barrier((mate_q[1], mo1))
    mo2, _ = attend(q_in, kv, False, True)
    back2 = lax.ppermute(mo2, "yr", SWAP)
    q_in, back1, mo2 = lax.optimization_barrier((qs[1], back1, mo2))
    o2, l2 = attend(q_in, kv, False, False)
    o = merge([(o1, l1, back1), (o2, l2, back2)])
    back = lax.all_to_all(o, seq, split_axis=0, concat_axis=0, tiled=True)
    here, back = lax.optimization_barrier((mine, back))
    back = back.reshape(mine.shape[:3] + (rows, HD))
    send = attended(here, other, back, True)
    came = lax.ppermute(send, "c", SWAP)
    keep = attended(here, other, back, False)
    return project(keep, came, out_weight, hidden, gate)[None]


def solution(mesh):
    devices = np.asarray(mesh.devices)
    fine = Mesh(devices.reshape(2, 2, 2, 2, 8, 2), ("xl", "c", "yv", "yr", "z", "xh"))
    view, seq = ("xl", "c"), ("yv", "yr", "z", "xh")
    spec = P(view, seq, None)
    return jax.shard_map(
        local,
        mesh=fine,
        in_specs=(spec, spec, spec, spec, P(), P(view, None)),
        out_specs=spec,
        check_vma=False,
    )
```

```python
import functools
import math

import jax
import jax.numpy as jnp
import numpy as np
from jax import lax
from jax.experimental import pallas as pl
from jax.experimental.pallas import tpu as pltpu
from jax.sharding import Mesh, PartitionSpec as P

HEADS = 16
HD = 128
BF = jnp.bfloat16
F32 = jnp.float32
SCALE = HD**-0.5
LOG2E = math.log2(math.e)
NT = (((1,), (1,)), ((), ()))
VMEM_CAP = 30 * 2**20


def params(**kw):
    return pltpu.CompilerParams(vmem_limit_bytes=VMEM_CAP, **kw)


def whole(n):
    return [pl.BlockSpec(memory_space=pltpu.VMEM)] * n


def fetch_half(core, refs, held, sems):
    half = held.shape[1]
    part = pl.ds(pl.multiple_of(core * half, half), half)
    moves = [
        pltpu.make_async_copy(ref.at[part], held.at[j], sems.at[j]) for j, ref in enumerate(refs)
    ]
    for move in moves:
        move.start()
    return moves


def pack_send_kernel(q_ref, k_ref, v_ref, sq_ref, sk_ref, sv_ref, held, sems):
    moves = fetch_half(1 - lax.axis_index("c"), (q_ref, k_ref, v_ref), held, sems)
    for j, out in enumerate((sq_ref, sk_ref, sv_ref)):
        moves[j].wait()
        for h in range(out.shape[1]):
            out[0, h] = held[j, :, h * HD : (h + 1) * HD]


def pack_keep_kernel(q_ref, k_ref, v_ref, o_ref, held, sems):
    me = lax.axis_index("c")
    moves = fetch_half(me, (q_ref, k_ref, v_ref), held, sems)
    for j in range(3):
        moves[j].wait()
        for h in range(o_ref.shape[2]):
            o_ref[me, 0, h, j] = held[j, :, h * HD : (h + 1) * HD]


def pack(kernel, out_shape, q, k, v):
    tok, width = q.shape
    return pl.pallas_call(
        kernel,
        in_specs=[pl.BlockSpec(memory_space=pltpu.HBM)] * 3,
        out_specs=whole(len(out_shape)),
        out_shape=[jax.ShapeDtypeStruct(x, BF) for x in out_shape],
        scratch_shapes=[pltpu.VMEM((3, tok // 2, width), BF), pltpu.SemaphoreType.DMA((3,))],
        compiler_params=params(),
        name="pack",
    )(*(pltpu.with_memory_space_constraint(x, pltpu.HBM) for x in (q, k, v)))


def place_kernel(a_ref, q_ref, k_ref, v_ref, o_ref):
    _, parts, heads = a_ref.shape[:3]
    you = 1 - lax.axis_index("c")
    for j, ref in enumerate((q_ref, k_ref, v_ref)):
        for r in range(parts):
            for h in range(heads):
                o_ref[you, r, h, j] = ref[r, h]


def place(mine, got):
    return pl.pallas_call(
        place_kernel,
        in_specs=whole(4),
        out_specs=pl.BlockSpec(memory_space=pltpu.VMEM),
        out_shape=jax.ShapeDtypeStruct(mine.shape, BF),
        input_output_aliases={0: 0},
        compiler_params=params(),
        name="place",
    )(mine, *got)


def gather_kv(kv_refs, k_all, v_all):
    at = 0
    for ref in kv_refs:
        n = ref.shape[0] * ref.shape[2]
        k_all[at : at + n, :] = ref[:, 0].reshape(n, HD)
        v_all[at : at + n, :HD] = ref[:, 1].reshape(n, HD)
        at += n
    v_all[:, HD:] = jnp.ones((at, HD), BF)


def eye():
    shape = (HD, HD)
    return lax.broadcasted_iota(jnp.int32, shape, 0) == lax.broadcasted_iota(jnp.int32, shape, 1)


def attend_block(q, k_all, v_all, kb):
    c = SCALE * LOG2E
    total = k_all.shape[0]

    def score(i):
        return lax.dot_general(q, k_all[i * kb : (i + 1) * kb, :], NT, preferred_element_type=F32)

    m = acc = None
    s = score(0)
    for i in range(total // kb):
        following = score(i + 1) if (i + 1) * kb < total else None
        peak = jnp.max(s, axis=1, keepdims=True) * c
        new = peak if m is None else jnp.maximum(m, peak)
        p = jnp.exp2(s * c - new).astype(BF)
        add = jnp.dot(p, v_all[i * kb : (i + 1) * kb, :], preferred_element_type=F32)
        acc = add if acc is None else acc * jnp.exp2(m - new) + add
        m, s = new, following
    return acc[:, :HD] / acc[:, HD:], m + jnp.log2(acc[:, HD:])


def attend_kernel(*refs, first, travels, qb, kb):
    if first:
        q_ref, *kv_refs, o_ref, l_ref, k_all, v_all = refs
        gather_kv(kv_refs, k_all, v_all)
    else:
        q_ref, k_all, v_all, o_ref, l_ref = refs
    src, rows, _ = q_ref.shape
    qsrc = qb // rows
    diag = eye()
    for j in range(src // qsrc):
        q = q_ref[j * qsrc : (j + 1) * qsrc].reshape(qb, HD)
        o, lse = attend_block(q, k_all, v_all, kb)
        o_ref[j * qsrc : (j + 1) * qsrc] = o.reshape(qsrc, rows, HD).astype(o_ref.dtype)
        for g in range(qb // HD):
            line = jnp.where(diag, lse[g * HD : (g + 1) * HD], 0.0)
            l_ref[j * (qb // HD) + g, :] = jnp.sum(line, axis=0)
    if travels:
        lines = l_ref.shape[0]
        lse = l_ref[...]
        terms = []
        for _ in range(3):
            terms.append(lse.astype(BF))
            lse = lse - terms[-1].astype(F32)
        terms.append(jnp.zeros((rows - 3 * lines, HD), BF))
        o_ref[src] = jnp.concatenate(terms, axis=0)


def attend(q, kv, first, travels, kb=2048):
    src, rows, _ = q.shape
    nq = src * rows
    qb = nq // 2
    total = sum(a.shape[0] * a.shape[2] for a in kv) if first else kv[0].shape[0]
    out_shape = [jax.ShapeDtypeStruct((src + travels, rows, HD), BF if travels else F32)]
    if not travels:
        out_shape.append(jax.ShapeDtypeStruct((nq // HD, HD), F32))
    if first:
        out_shape += [
            jax.ShapeDtypeStruct((total, HD), BF),
            jax.ShapeDtypeStruct((total, 2 * HD), BF),
        ]
    return pl.pallas_call(
        functools.partial(attend_kernel, first=first, travels=travels, qb=qb, kb=min(kb, total)),
        in_specs=whole(1 + len(kv)),
        out_specs=whole(len(out_shape)),
        out_shape=out_shape,
        scratch_shapes=[pltpu.VMEM((nq // HD, HD), F32)] if travels else [],
        compiler_params=params(),
        cost_estimate=pl.CostEstimate(
            flops=0,
            bytes_accessed=0,
            transcendentals=0,
        ),
        name="attend",
    )(q, *kv)


def merge_kernel(*refs, own_parts):
    *refs, out_ref = refs
    diag = eye()
    rows = out_ref.shape[1]
    per = HD // rows
    here, there = [], []
    for o_ref, l_ref in zip(refs[: 2 * own_parts : 2], refs[1 : 2 * own_parts : 2]):
        for g in range(l_ref.shape[0]):
            here.append((o_ref, g, l_ref[g : g + 1, :]))
    for o_ref in refs[2 * own_parts :]:
        src = o_ref.shape[0] - 1
        lines = src // per
        terms = o_ref[src].astype(F32)
        lse = terms[:lines] + terms[lines : 2 * lines] + terms[2 * lines : 3 * lines]
        for g in range(lines):
            there.append((o_ref, g, lse[g : g + 1, :]))
    for i, ((oa, ga, la), (ob, gb, lb)) in enumerate(zip(here, there)):
        peak = jnp.maximum(la, lb)
        ea, eb = jnp.exp2(la - peak), jnp.exp2(lb - peak)
        w = jnp.sum(jnp.where(diag, ea / (ea + eb), 0.0), axis=1, keepdims=True)
        a = oa[ga * per : (ga + 1) * per].reshape(HD, HD)
        b = ob[gb * per : (gb + 1) * per].reshape(HD, HD).astype(F32)
        out_ref[i * per : (i + 1) * per] = (b + w * (a - b)).astype(BF).reshape(per, rows, HD)


def merge(own, travelled):
    src = sum(o.shape[0] for o, _ in own)
    flat = [x for p in own for x in p] + travelled
    return pl.pallas_call(
        functools.partial(merge_kernel, own_parts=len(own)),
        in_specs=whole(len(flat)),
        out_specs=pl.BlockSpec(memory_space=pltpu.VMEM),
        out_shape=jax.ShapeDtypeStruct((src,) + own[0][0].shape[1:], BF),
        compiler_params=params(),
        name="merge",
    )(*flat)


def cross_kernel(a_ref, b_ref, *refs, flip):
    *s_ref, o_ref = refs
    views, parts, heads = a_ref.shape[:3]
    view = lax.axis_index("c")
    if flip:
        view = 1 - view

    def one_head(h, carry):
        for r in range(parts):
            ks = [a_ref[b, r, h, 1].astype(F32) for b in range(views)]
            ks += [b_ref[b, r, h, 0].astype(F32) for b in range(views)]
            vs = [a_ref[b, r, h, 2].astype(F32) for b in range(views)]
            vs += [b_ref[b, r, h, 1].astype(F32) for b in range(views)]
            q = a_ref[view, r, h, 0].astype(F32)
            s = [jnp.sum(q * k, axis=1, keepdims=True) * SCALE for k in ks]
            peak = functools.reduce(jnp.maximum, s)
            e = [jnp.exp(x - peak) for x in s]
            inv = 1.0 / functools.reduce(jnp.add, e)
            terms = [(x * inv).astype(BF).astype(F32) * v for x, v in zip(e, vs)]
            out = functools.reduce(jnp.add, terms)
            if s_ref:
                out = s_ref[0][view, r, h].astype(F32) + out
            o_ref[r, h] = out.astype(o_ref.dtype)
        return carry

    lax.fori_loop(0, heads, one_head, 0, unroll=8)


def cross(mine, other, back, flip):
    args = (mine, other) if back is None else (mine, other, back)
    out = jax.ShapeDtypeStruct(mine.shape[1:3] + mine.shape[4:], F32 if back is None else BF)
    return pl.pallas_call(
        functools.partial(cross_kernel, flip=flip),
        in_specs=whole(len(args)),
        out_specs=pl.BlockSpec(memory_space=pltpu.VMEM),
        out_shape=out,
        compiler_params=params(),
        name="cross",
    )(*args)


def add_kernel(s_ref, c_ref, o_ref):
    o_ref[...] = (s_ref[1 - lax.axis_index("c")].astype(F32) + c_ref[...]).astype(BF)


def add_send(back, cross_out):
    return pl.pallas_call(
        add_kernel,
        in_specs=whole(2),
        out_specs=pl.BlockSpec(memory_space=pltpu.VMEM),
        out_shape=jax.ShapeDtypeStruct(cross_out.shape, BF),
        compiler_params=params(),
        name="add_send",
    )(back, cross_out)


def project_kernel(keep_ref, came_ref, w_ref, h_ref, g_ref, o_ref, att):
    half = o_ref.shape[0] // 2
    me = lax.axis_index("c")
    for core, ref in ((me, keep_ref), (1 - me, came_ref)):
        parts, heads, rows, _ = ref.shape
        for r in range(parts):
            at = pl.ds(pl.multiple_of(core * half + r * rows, rows), rows)
            for h in range(heads):
                att[at, h * HD : (h + 1) * HD] = ref[r, h]
    nb = 512
    for i in range(o_ref.shape[1] // nb):
        cols = slice(i * nb, (i + 1) * nb)
        y = jnp.dot(att[...], w_ref[:, cols], preferred_element_type=F32)
        o_ref[:, cols] = (h_ref[:, cols].astype(F32) + g_ref[:, cols].astype(F32) * y).astype(BF)


def project(keep, came, w, hidden, gate):
    return pl.pallas_call(
        project_kernel,
        in_specs=whole(5),
        out_specs=pl.BlockSpec(memory_space=pltpu.VMEM),
        out_shape=jax.ShapeDtypeStruct(hidden.shape, BF),
        scratch_shapes=[pltpu.VMEM(hidden.shape, BF)],
        compiler_params=params(),
        name="project",
    )(keep, came, w, hidden, gate)


SWAP = [(0, 1), (1, 0)]
CHUNKS = 2


def swap(chunks, axis):
    return [lax.ppermute(x, axis, SWAP) for x in chunks]


def local(hidden_in, queries, keys, values, out_weight, gate):
    hidden, q, k, v = hidden_in[0], queries[0], keys[0], values[0]
    tok, _ = q.shape
    seq = ("yv", "z", "xh")
    rows = tok // 2
    n = 2 * HEADS

    away = pack(pack_send_kernel, [(1, HEADS, rows, HD)] * 3, q, k, v)
    came = swap(away, "c")
    (mine,) = pack(pack_keep_kernel, [(2, 1, HEADS, 3, rows, HD)], q, k, v)
    mine = place(mine, came)
    got = lax.all_to_all(mine.reshape(n, 3 * rows, HD), seq, split_axis=0, concat_axis=0, tiled=True)
    got = got.reshape(n, 3, rows, HD)

    step, half, lead = n // CHUNKS, n // 2, n * 5 // 8
    own = [got[i * step : (i + 1) * step, 1:] for i in range(CHUNKS)]
    own_pair = swap(own, "c")
    q_first, q_last = got[:lead, 0], got[lead:, 0]
    here, got = lax.optimization_barrier((mine, got))
    other = lax.ppermute(here[:, :, :, 1:], "xl", SWAP)
    mate_q = swap([got[:half, 0], got[half:, 0]], "yr")

    o1, l1, keys_all, values_all = attend(q_first, own + own_pair, True, False)
    kv = keys_all, values_all
    q_in, o1 = lax.optimization_barrier((mate_q[0], o1))
    (mo1,) = attend(q_in, kv, False, True)
    back1 = lax.ppermute(mo1, "yr", SWAP)
    q_in, mo1 = lax.optimization_barrier((mate_q[1], mo1))
    (mo2,) = attend(q_in, kv, False, True)
    back2 = lax.ppermute(mo2, "yr", SWAP)
    q_in, back1, mo2 = lax.optimization_barrier((q_last, back1, mo2))
    o2, l2 = attend(q_in, kv, False, False)
    other, o2 = lax.optimization_barrier((other, o2))
    cross_send = cross(mine, other, None, True)
    back2, cross_send = lax.optimization_barrier((back2, cross_send))
    o = merge([(o1, l1), (o2, l2)], [back1, back2])
    back = lax.all_to_all(o, seq, split_axis=0, concat_axis=0, tiled=True)
    here, back = lax.optimization_barrier((mine, back))
    back = back.reshape(mine.shape[:3] + (rows, HD))
    send = add_send(back, cross_send)
    came = lax.ppermute(send, "c", SWAP)
    keep = cross(here, other, back, False)
    return project(keep, came, out_weight, hidden, gate)[None]


def solution(mesh):
    devices = np.asarray(mesh.devices)
    fine = Mesh(devices.reshape(2, 2, 2, 2, 8, 2), ("xl", "c", "yv", "yr", "z", "xh"))
    view, seq = ("xl", "c"), ("yv", "yr", "z", "xh")
    spec = P(view, seq, None)
    return jax.shard_map(
        local,
        mesh=fine,
        in_specs=(spec, spec, spec, spec, P(), P(view, None)),
        out_specs=spec,
        check_vma=False,
    )
```

```python
import functools
import math

import jax
import jax.numpy as jnp
import numpy as np
from jax import lax
from jax.experimental import pallas as pl
from jax.experimental.pallas import tpu as pltpu
from jax.sharding import Mesh, PartitionSpec as P

HEADS = 16
HD = 128
BF = jnp.bfloat16
F32 = jnp.float32
SCALE = HD**-0.5
LOG2E = math.log2(math.e)
NT = (((1,), (1,)), ((), ()))
VMEM_CAP = 30 * 2**20


def params(**kw):
    return pltpu.CompilerParams(vmem_limit_bytes=VMEM_CAP, **kw)


def whole(n):
    return [pl.BlockSpec(memory_space=pltpu.VMEM)] * n


def fetch_half(core, refs, held, sems):
    half = held.shape[1]
    part = pl.ds(pl.multiple_of(core * half, half), half)
    moves = [
        pltpu.make_async_copy(ref.at[part], held.at[j], sems.at[j]) for j, ref in enumerate(refs)
    ]
    for move in moves:
        move.start()
    return moves


def pack_send_kernel(q_ref, k_ref, v_ref, sq_ref, sk_ref, sv_ref, held, sems):
    moves = fetch_half(1 - lax.axis_index("c"), (q_ref, k_ref, v_ref), held, sems)
    for j, out in enumerate((sq_ref, sk_ref, sv_ref)):
        moves[j].wait()
        for h in range(out.shape[1]):
            out[0, h] = held[j, :, h * HD : (h + 1) * HD]


def pack_keep_kernel(q_ref, k_ref, v_ref, o_ref, held, sems):
    me = lax.axis_index("c")
    moves = fetch_half(me, (q_ref, k_ref, v_ref), held, sems)
    for j in range(3):
        moves[j].wait()
        for h in range(o_ref.shape[2]):
            o_ref[me, 0, h, j] = held[j, :, h * HD : (h + 1) * HD]


def pack(kernel, out_shape, q, k, v):
    tok, width = q.shape
    return pl.pallas_call(
        kernel,
        in_specs=[pl.BlockSpec(memory_space=pltpu.HBM)] * 3,
        out_specs=whole(len(out_shape)),
        out_shape=[jax.ShapeDtypeStruct(x, BF) for x in out_shape],
        scratch_shapes=[pltpu.VMEM((3, tok // 2, width), BF), pltpu.SemaphoreType.DMA((3,))],
        compiler_params=params(),
        name="pack",
    )(*(pltpu.with_memory_space_constraint(x, pltpu.HBM) for x in (q, k, v)))


def place_kernel(a_ref, q_ref, k_ref, v_ref, o_ref):
    _, parts, heads = a_ref.shape[:3]
    you = 1 - lax.axis_index("c")
    for j, ref in enumerate((q_ref, k_ref, v_ref)):
        for r in range(parts):
            for h in range(heads):
                o_ref[you, r, h, j] = ref[r, h]


def place(mine, got):
    return pl.pallas_call(
        place_kernel,
        in_specs=whole(4),
        out_specs=pl.BlockSpec(memory_space=pltpu.VMEM),
        out_shape=jax.ShapeDtypeStruct(mine.shape, BF),
        input_output_aliases={0: 0},
        compiler_params=params(),
        name="place",
    )(mine, *got)


def gather_kv(kv_refs, k_all, v_all):
    at = 0
    for ref in kv_refs:
        n = ref.shape[0] * ref.shape[2]
        k_all[at : at + n, :] = ref[:, 0].reshape(n, HD)
        v_all[at : at + n, :HD] = ref[:, 1].reshape(n, HD)
        at += n
    v_all[:, HD:] = jnp.ones((at, HD), BF)


def eye():
    shape = (HD, HD)
    return lax.broadcasted_iota(jnp.int32, shape, 0) == lax.broadcasted_iota(jnp.int32, shape, 1)


def attend_block(q, k_all, v_all, kb):
    c = SCALE * LOG2E
    total = k_all.shape[0]

    def score(i):
        return lax.dot_general(q, k_all[i * kb : (i + 1) * kb, :], NT, preferred_element_type=F32)

    m = acc = None
    s = score(0)
    for i in range(total // kb):
        following = score(i + 1) if (i + 1) * kb < total else None
        peak = jnp.max(s, axis=1, keepdims=True) * c
        new = peak if m is None else jnp.maximum(m, peak)
        p = jnp.exp2(s * c - new).astype(BF)
        add = jnp.dot(p, v_all[i * kb : (i + 1) * kb, :], preferred_element_type=F32)
        acc = add if acc is None else acc * jnp.exp2(m - new) + add
        m, s = new, following
    return acc[:, :HD] / acc[:, HD:], m + jnp.log2(acc[:, HD:])


def attend_kernel(*refs, first, travels, qb, kb):
    if first:
        q_ref, *kv_refs, o_ref, l_ref, k_all, v_all = refs
        gather_kv(kv_refs, k_all, v_all)
    else:
        q_ref, k_all, v_all, o_ref, l_ref = refs
    src, rows, _ = q_ref.shape
    qsrc = qb // rows
    diag = eye()
    for j in range(src // qsrc):
        q = q_ref[j * qsrc : (j + 1) * qsrc].reshape(qb, HD)
        o, lse = attend_block(q, k_all, v_all, kb)
        o_ref[j * qsrc : (j + 1) * qsrc] = o.reshape(qsrc, rows, HD).astype(o_ref.dtype)
        for g in range(qb // HD):
            line = jnp.where(diag, lse[g * HD : (g + 1) * HD], 0.0)
            l_ref[j * (qb // HD) + g, :] = jnp.sum(line, axis=0)
    if travels:
        lines = l_ref.shape[0]
        lse = l_ref[...]
        terms = []
        for _ in range(3):
            terms.append(lse.astype(BF))
            lse = lse - terms[-1].astype(F32)
        terms.append(jnp.zeros((rows - 3 * lines, HD), BF))
        o_ref[src] = jnp.concatenate(terms, axis=0)


def attend(q, kv, first, travels, kb=2048):
    src, rows, _ = q.shape
    nq = src * rows
    qb = nq // 2
    total = sum(a.shape[0] * a.shape[2] for a in kv) if first else kv[0].shape[0]
    out_shape = [jax.ShapeDtypeStruct((src + travels, rows, HD), BF if travels else F32)]
    if not travels:
        out_shape.append(jax.ShapeDtypeStruct((nq // HD, HD), F32))
    if first:
        out_shape += [
            jax.ShapeDtypeStruct((total, HD), BF),
            jax.ShapeDtypeStruct((total, 2 * HD), BF),
        ]
    return pl.pallas_call(
        functools.partial(attend_kernel, first=first, travels=travels, qb=qb, kb=min(kb, total)),
        in_specs=whole(1 + len(kv)),
        out_specs=whole(len(out_shape)),
        out_shape=out_shape,
        scratch_shapes=[pltpu.VMEM((nq // HD, HD), F32)] if travels else [],
        compiler_params=params(),
        cost_estimate=pl.CostEstimate(
            flops=0,
            bytes_accessed=0,
            transcendentals=0,
        ),
        name="attend",
    )(q, *kv)


def merge_kernel(*refs, own_parts):
    *refs, out_ref = refs
    diag = eye()
    rows = out_ref.shape[1]
    per = HD // rows
    here, there = [], []
    for o_ref, l_ref in zip(refs[: 2 * own_parts : 2], refs[1 : 2 * own_parts : 2]):
        for g in range(l_ref.shape[0]):
            here.append((o_ref, g, l_ref[g : g + 1, :]))
    for o_ref in refs[2 * own_parts :]:
        src = o_ref.shape[0] - 1
        lines = src // per
        terms = o_ref[src].astype(F32)
        lse = terms[:lines] + terms[lines : 2 * lines] + terms[2 * lines : 3 * lines]
        for g in range(lines):
            there.append((o_ref, g, lse[g : g + 1, :]))
    for i, ((oa, ga, la), (ob, gb, lb)) in enumerate(zip(here, there)):
        peak = jnp.maximum(la, lb)
        ea, eb = jnp.exp2(la - peak), jnp.exp2(lb - peak)
        w = jnp.sum(jnp.where(diag, ea / (ea + eb), 0.0), axis=1, keepdims=True)
        a = oa[ga * per : (ga + 1) * per].reshape(HD, HD)
        b = ob[gb * per : (gb + 1) * per].reshape(HD, HD).astype(F32)
        out_ref[i * per : (i + 1) * per] = (b + w * (a - b)).astype(BF).reshape(per, rows, HD)


def merge(own, travelled):
    src = sum(o.shape[0] for o, _ in own)
    flat = [x for p in own for x in p] + travelled
    return pl.pallas_call(
        functools.partial(merge_kernel, own_parts=len(own)),
        in_specs=whole(len(flat)),
        out_specs=pl.BlockSpec(memory_space=pltpu.VMEM),
        out_shape=jax.ShapeDtypeStruct((src,) + own[0][0].shape[1:], BF),
        compiler_params=params(),
        name="merge",
    )(*flat)


def cross_kernel(a_ref, b_ref, *refs, flip):
    *s_ref, o_ref = refs
    views, parts, heads = a_ref.shape[:3]
    view = lax.axis_index("c")
    if flip:
        view = 1 - view

    def one_head(h, carry):
        for r in range(parts):
            ks = [a_ref[b, r, h, 1].astype(F32) for b in range(views)]
            ks += [b_ref[b, r, h, 0].astype(F32) for b in range(views)]
            vs = [a_ref[b, r, h, 2].astype(F32) for b in range(views)]
            vs += [b_ref[b, r, h, 1].astype(F32) for b in range(views)]
            q = a_ref[view, r, h, 0].astype(F32)
            s = [jnp.sum(q * k, axis=1, keepdims=True) * SCALE for k in ks]
            peak = functools.reduce(jnp.maximum, s)
            e = [jnp.exp(x - peak) for x in s]
            inv = 1.0 / functools.reduce(jnp.add, e)
            terms = [(x * inv).astype(BF).astype(F32) * v for x, v in zip(e, vs)]
            out = functools.reduce(jnp.add, terms)
            if s_ref:
                out = s_ref[0][view, r, h].astype(F32) + out
            o_ref[r, h] = out.astype(o_ref.dtype)
        return carry

    lax.fori_loop(0, heads, one_head, 0, unroll=8)


def cross(mine, other, back, flip):
    args = (mine, other) if back is None else (mine, other, back)
    out = jax.ShapeDtypeStruct(mine.shape[1:3] + mine.shape[4:], F32 if back is None else BF)
    return pl.pallas_call(
        functools.partial(cross_kernel, flip=flip),
        in_specs=whole(len(args)),
        out_specs=pl.BlockSpec(memory_space=pltpu.VMEM),
        out_shape=out,
        compiler_params=params(),
        name="cross",
    )(*args)


def add_kernel(s_ref, c_ref, o_ref):
    o_ref[...] = (s_ref[1 - lax.axis_index("c")].astype(F32) + c_ref[...]).astype(BF)


def add_send(back, cross_out):
    return pl.pallas_call(
        add_kernel,
        in_specs=whole(2),
        out_specs=pl.BlockSpec(memory_space=pltpu.VMEM),
        out_shape=jax.ShapeDtypeStruct(cross_out.shape, BF),
        compiler_params=params(),
        name="add_send",
    )(back, cross_out)


def project_kernel(keep_ref, came_ref, w_ref, h_ref, g_ref, o_ref, att):
    half = o_ref.shape[0] // 2
    me = lax.axis_index("c")
    for core, ref in ((me, keep_ref), (1 - me, came_ref)):
        parts, heads, rows, _ = ref.shape
        for r in range(parts):
            at = pl.ds(pl.multiple_of(core * half + r * rows, rows), rows)
            for h in range(heads):
                att[at, h * HD : (h + 1) * HD] = ref[r, h]
    nb = 512
    for i in range(o_ref.shape[1] // nb):
        cols = slice(i * nb, (i + 1) * nb)
        y = jnp.dot(att[...], w_ref[:, cols], preferred_element_type=F32)
        o_ref[:, cols] = (h_ref[:, cols].astype(F32) + g_ref[:, cols].astype(F32) * y).astype(BF)


def project(keep, came, w, hidden, gate):
    return pl.pallas_call(
        project_kernel,
        in_specs=whole(5),
        out_specs=pl.BlockSpec(memory_space=pltpu.VMEM),
        out_shape=jax.ShapeDtypeStruct(hidden.shape, BF),
        scratch_shapes=[pltpu.VMEM(hidden.shape, BF)],
        compiler_params=params(),
        name="project",
    )(keep, came, w, hidden, gate)


SWAP = [(0, 1), (1, 0)]
CHUNKS = 2


def swap(chunks, axis):
    return [lax.ppermute(x, axis, SWAP) for x in chunks]


def local(hidden_in, queries, keys, values, out_weight, gate):
    hidden, q, k, v = hidden_in[0], queries[0], keys[0], values[0]
    tok, _ = q.shape
    seq = ("yv", "z", "xh")
    rows = tok // 2
    n = 2 * HEADS

    away = pack(pack_send_kernel, [(1, HEADS, rows, HD)] * 3, q, k, v)
    came = swap(away, "c")
    (mine,) = pack(pack_keep_kernel, [(2, 1, HEADS, 3, rows, HD)], q, k, v)
    mine = place(mine, came)
    got = lax.all_to_all(mine.reshape(n, 3 * rows, HD), seq, split_axis=0, concat_axis=0, tiled=True)
    got = got.reshape(n, 3, rows, HD)

    step, half = n // CHUNKS, n // 2
    own = [got[i * step : (i + 1) * step, 1:] for i in range(CHUNKS)]
    own_pair = swap(own, "c")
    qs = [got[a * n // 4 : b * n // 4, 0] for a, b in ((0, 1), (1, 2), (2, 4))]
    here, got = lax.optimization_barrier((mine, got))
    other = lax.ppermute(here[:, :, :, 1:], "xl", SWAP)
    mate_q1 = lax.ppermute(got[:half, 0], "yr", SWAP)

    o1, l1, keys_all, values_all = attend(qs[0], own + own_pair, True, False)
    kv = keys_all, values_all
    q_in, q2, o1 = lax.optimization_barrier((qs[1], got[half:, 0], o1))
    mate_q2 = lax.ppermute(q2, "yr", SWAP)
    o2, l2 = attend(q_in, kv, False, False)
    q_in, o2 = lax.optimization_barrier((mate_q1, o2))
    (mo1,) = attend(q_in, kv, False, True)
    back1 = lax.ppermute(mo1, "yr", SWAP)
    q_in, mo1 = lax.optimization_barrier((mate_q2, mo1))
    (mo2,) = attend(q_in, kv, False, True)
    back2 = lax.ppermute(mo2, "yr", SWAP)
    q_in, back1, mo2 = lax.optimization_barrier((qs[2], back1, mo2))
    o3, l3 = attend(q_in, kv, False, False)
    other, o3 = lax.optimization_barrier((other, o3))
    cross_send = cross(mine, other, None, True)
    back2, cross_send = lax.optimization_barrier((back2, cross_send))
    o = merge([(o1, l1), (o2, l2), (o3, l3)], [back1, back2])
    back = lax.all_to_all(o, seq, split_axis=0, concat_axis=0, tiled=True)
    here, back = lax.optimization_barrier((mine, back))
    back = back.reshape(mine.shape[:3] + (rows, HD))
    send = add_send(back, cross_send)
    came = lax.ppermute(send, "c", SWAP)
    keep = cross(here, other, back, False)
    return project(keep, came, out_weight, hidden, gate)[None]


def solution(mesh):
    devices = np.asarray(mesh.devices)
    fine = Mesh(devices.reshape(2, 2, 2, 2, 8, 2), ("xl", "c", "yv", "yr", "z", "xh"))
    view, seq = ("xl", "c"), ("yv", "yr", "z", "xh")
    spec = P(view, seq, None)
    return jax.shard_map(
        local,
        mesh=fine,
        in_specs=(spec, spec, spec, spec, P(), P(view, None)),
        out_specs=spec,
        check_vma=False,
    )
```

```python
import functools
import math

import jax
import jax.numpy as jnp
import numpy as np
from jax import lax
from jax.experimental import pallas as pl
from jax.experimental.pallas import tpu as pltpu
from jax.sharding import Mesh, PartitionSpec as P

HEADS = 16
HD = 128
BF = jnp.bfloat16
F32 = jnp.float32
SCALE = HD**-0.5
LOG2E = math.log2(math.e)
NT = (((1,), (1,)), ((), ()))
VMEM_CAP = 30 * 2**20


def params(**kw):
    return pltpu.CompilerParams(vmem_limit_bytes=VMEM_CAP, **kw)


def whole(n):
    return [pl.BlockSpec(memory_space=pltpu.VMEM)] * n


def fetch_half(core, refs, held, sems):
    half = held.shape[1]
    part = pl.ds(pl.multiple_of(core * half, half), half)
    moves = [
        pltpu.make_async_copy(ref.at[part], held.at[j], sems.at[j]) for j, ref in enumerate(refs)
    ]
    for move in moves:
        move.start()
    return moves


def pack_send_kernel(q_ref, k_ref, v_ref, o_ref, held, sems):
    moves = fetch_half(1 - lax.axis_index("c"), (q_ref, k_ref, v_ref), held, sems)
    for j in range(3):
        moves[j].wait()
        for h in range(o_ref.shape[1]):
            o_ref[j, h] = held[j, :, h * HD : (h + 1) * HD]


def pack_keep_kernel(q_ref, k_ref, v_ref, o_ref, held, sems):
    me = lax.axis_index("c")
    moves = fetch_half(me, (q_ref, k_ref, v_ref), held, sems)
    for j in range(3):
        moves[j].wait()
        for h in range(o_ref.shape[2]):
            o_ref[me, 0, h, j] = held[j, :, h * HD : (h + 1) * HD]


def pack(kernel, out_shape, q, k, v):
    tok, width = q.shape
    return pl.pallas_call(
        kernel,
        in_specs=[pl.BlockSpec(memory_space=pltpu.HBM)] * 3,
        out_specs=whole(len(out_shape)),
        out_shape=[jax.ShapeDtypeStruct(x, BF) for x in out_shape],
        scratch_shapes=[pltpu.VMEM((3, tok // 2, width), BF), pltpu.SemaphoreType.DMA((3,))],
        compiler_params=params(),
        name="pack",
    )(*(pltpu.with_memory_space_constraint(x, pltpu.HBM) for x in (q, k, v)))


def place_kernel(a_ref, got_ref, o_ref):
    you = 1 - lax.axis_index("c")
    for j in range(got_ref.shape[0]):
        for h in range(got_ref.shape[1]):
            o_ref[you, 0, h, j] = got_ref[j, h]


def place(mine, got):
    return pl.pallas_call(
        place_kernel,
        in_specs=whole(2),
        out_specs=pl.BlockSpec(memory_space=pltpu.VMEM),
        out_shape=jax.ShapeDtypeStruct(mine.shape, BF),
        input_output_aliases={0: 0},
        compiler_params=params(),
        name="place",
    )(mine, got)


def gather_kv(kv_refs, k_all, v_all):
    at = 0
    for ref in kv_refs:
        n = ref.shape[0] * ref.shape[2]
        k_all[at : at + n, :] = ref[:, 0].reshape(n, HD)
        v_all[at : at + n, :HD] = ref[:, 1].reshape(n, HD)
        at += n
    v_all[:, HD:] = jnp.ones((at, HD), BF)


def eye():
    shape = (HD, HD)
    return lax.broadcasted_iota(jnp.int32, shape, 0) == lax.broadcasted_iota(jnp.int32, shape, 1)


def attend_block(q, k_all, v_all, kb):
    c = SCALE * LOG2E
    total = k_all.shape[0]

    def score(i):
        return lax.dot_general(q, k_all[i * kb : (i + 1) * kb, :], NT, preferred_element_type=F32)

    m = acc = None
    s = score(0)
    for i in range(total // kb):
        following = score(i + 1) if (i + 1) * kb < total else None
        peak = jnp.max(s, axis=1, keepdims=True) * c
        new = peak if m is None else jnp.maximum(m, peak)
        p = jnp.exp2(s * c - new).astype(BF)
        add = jnp.dot(p, v_all[i * kb : (i + 1) * kb, :], preferred_element_type=F32)
        acc = add if acc is None else acc * jnp.exp2(m - new) + add
        m, s = new, following
    return acc[:, :HD] / acc[:, HD:], m + jnp.log2(acc[:, HD:])


def attend_kernel(*refs, first, travels, qb, kb):
    if first:
        q_ref, *kv_refs, o_ref, l_ref, k_all, v_all = refs
        gather_kv(kv_refs, k_all, v_all)
    else:
        q_ref, k_all, v_all, o_ref, l_ref = refs
    src, rows, _ = q_ref.shape
    qsrc = qb // rows
    diag = eye()
    for j in range(src // qsrc):
        q = q_ref[j * qsrc : (j + 1) * qsrc].reshape(qb, HD)
        o, lse = attend_block(q, k_all, v_all, kb)
        o_ref[j * qsrc : (j + 1) * qsrc] = o.reshape(qsrc, rows, HD).astype(o_ref.dtype)
        for g in range(qb // HD):
            line = jnp.where(diag, lse[g * HD : (g + 1) * HD], 0.0)
            l_ref[j * (qb // HD) + g, :] = jnp.sum(line, axis=0)
    if travels:
        lines = l_ref.shape[0]
        lse = l_ref[...]
        terms = []
        for _ in range(3):
            terms.append(lse.astype(BF))
            lse = lse - terms[-1].astype(F32)
        terms.append(jnp.zeros((rows - 3 * lines, HD), BF))
        o_ref[src] = jnp.concatenate(terms, axis=0)


def attend(q, kv, first, travels, kb=2048):
    src, rows, _ = q.shape
    nq = src * rows
    qb = nq if nq <= 512 else nq // 2
    total = sum(a.shape[0] * a.shape[2] for a in kv) if first else kv[0].shape[0]
    out_shape = [jax.ShapeDtypeStruct((src + travels, rows, HD), BF if travels else F32)]
    if not travels:
        out_shape.append(jax.ShapeDtypeStruct((nq // HD, HD), F32))
    if first:
        out_shape += [
            jax.ShapeDtypeStruct((total, HD), BF),
            jax.ShapeDtypeStruct((total, 2 * HD), BF),
        ]
    return pl.pallas_call(
        functools.partial(attend_kernel, first=first, travels=travels, qb=qb, kb=min(kb, total)),
        in_specs=whole(1 + len(kv)),
        out_specs=whole(len(out_shape)),
        out_shape=out_shape,
        scratch_shapes=[pltpu.VMEM((nq // HD, HD), F32)] if travels else [],
        compiler_params=params(),
        cost_estimate=pl.CostEstimate(
            flops=0,
            bytes_accessed=0,
            transcendentals=0,
        ),
        name="attend",
    )(q, *kv)


def merge_kernel(*refs, own_parts):
    *refs, out_ref = refs
    diag = eye()
    rows = out_ref.shape[1]
    per = HD // rows
    here, there = [], []
    for o_ref, l_ref in zip(refs[: 2 * own_parts : 2], refs[1 : 2 * own_parts : 2]):
        for g in range(l_ref.shape[0]):
            here.append((o_ref, g, l_ref[g : g + 1, :]))
    for o_ref in refs[2 * own_parts :]:
        src = o_ref.shape[0] - 1
        lines = src // per
        terms = o_ref[src].astype(F32)
        lse = terms[:lines] + terms[lines : 2 * lines] + terms[2 * lines : 3 * lines]
        for g in range(lines):
            there.append((o_ref, g, lse[g : g + 1, :]))
    for i, ((oa, ga, la), (ob, gb, lb)) in enumerate(zip(here, there)):
        peak = jnp.maximum(la, lb)
        ea, eb = jnp.exp2(la - peak), jnp.exp2(lb - peak)
        w = jnp.sum(jnp.where(diag, ea / (ea + eb), 0.0), axis=1, keepdims=True)
        a = oa[ga * per : (ga + 1) * per].reshape(HD, HD)
        b = ob[gb * per : (gb + 1) * per].reshape(HD, HD).astype(F32)
        out_ref[i * per : (i + 1) * per] = (b + w * (a - b)).astype(BF).reshape(per, rows, HD)


def merge(own, travelled):
    src = sum(o.shape[0] for o, _ in own)
    flat = [x for p in own for x in p] + travelled
    return pl.pallas_call(
        functools.partial(merge_kernel, own_parts=len(own)),
        in_specs=whole(len(flat)),
        out_specs=pl.BlockSpec(memory_space=pltpu.VMEM),
        out_shape=jax.ShapeDtypeStruct((src,) + own[0][0].shape[1:], BF),
        compiler_params=params(),
        name="merge",
    )(*flat)


def cross_kernel(a_ref, b_ref, *refs, flip):
    *s_ref, o_ref = refs
    views, parts, heads = a_ref.shape[:3]
    view = lax.axis_index("c")
    if flip:
        view = 1 - view

    def one_head(h, carry):
        for r in range(parts):
            ks = [a_ref[b, r, h, 1].astype(F32) for b in range(views)]
            ks += [b_ref[b, r, h, 0].astype(F32) for b in range(views)]
            vs = [a_ref[b, r, h, 2].astype(F32) for b in range(views)]
            vs += [b_ref[b, r, h, 1].astype(F32) for b in range(views)]
            q = a_ref[view, r, h, 0].astype(F32)
            s = [jnp.sum(q * k, axis=1, keepdims=True) * SCALE for k in ks]
            peak = functools.reduce(jnp.maximum, s)
            e = [jnp.exp(x - peak) for x in s]
            inv = 1.0 / functools.reduce(jnp.add, e)
            terms = [(x * inv).astype(BF).astype(F32) * v for x, v in zip(e, vs)]
            out = functools.reduce(jnp.add, terms)
            if s_ref:
                out = s_ref[0][view, r, h].astype(F32) + out
            o_ref[r, h] = out.astype(o_ref.dtype)
        return carry

    lax.fori_loop(0, heads, one_head, 0, unroll=8)


def cross(mine, other, back, flip):
    args = (mine, other) if back is None else (mine, other, back)
    out = jax.ShapeDtypeStruct(mine.shape[1:3] + mine.shape[4:], F32 if back is None else BF)
    return pl.pallas_call(
        functools.partial(cross_kernel, flip=flip),
        in_specs=whole(len(args)),
        out_specs=pl.BlockSpec(memory_space=pltpu.VMEM),
        out_shape=out,
        compiler_params=params(),
        name="cross",
    )(*args)


def add_kernel(s_ref, c_ref, o_ref):
    o_ref[...] = (s_ref[1 - lax.axis_index("c")].astype(F32) + c_ref[...]).astype(BF)


def add_send(back, cross_out):
    return pl.pallas_call(
        add_kernel,
        in_specs=whole(2),
        out_specs=pl.BlockSpec(memory_space=pltpu.VMEM),
        out_shape=jax.ShapeDtypeStruct(cross_out.shape, BF),
        compiler_params=params(),
        name="add_send",
    )(back, cross_out)


def project_kernel(keep_ref, came_ref, w_ref, h_ref, g_ref, o_ref, att):
    half = o_ref.shape[0] // 2
    me = lax.axis_index("c")
    for core, ref in ((me, keep_ref), (1 - me, came_ref)):
        parts, heads, rows, _ = ref.shape
        for r in range(parts):
            at = pl.ds(pl.multiple_of(core * half + r * rows, rows), rows)
            for h in range(heads):
                att[at, h * HD : (h + 1) * HD] = ref[r, h]
    nb = 512
    for i in range(o_ref.shape[1] // nb):
        cols = slice(i * nb, (i + 1) * nb)
        y = jnp.dot(att[...], w_ref[:, cols], preferred_element_type=F32)
        o_ref[:, cols] = (h_ref[:, cols].astype(F32) + g_ref[:, cols].astype(F32) * y).astype(BF)


def project(keep, came, w, hidden, gate):
    return pl.pallas_call(
        project_kernel,
        in_specs=whole(5),
        out_specs=pl.BlockSpec(memory_space=pltpu.VMEM),
        out_shape=jax.ShapeDtypeStruct(hidden.shape, BF),
        scratch_shapes=[pltpu.VMEM(hidden.shape, BF)],
        compiler_params=params(),
        name="project",
    )(keep, came, w, hidden, gate)


SWAP = [(0, 1), (1, 0)]
CHUNKS = 1


def swap(chunks, axis):
    return [lax.ppermute(x, axis, SWAP) for x in chunks]


def local(hidden_in, queries, keys, values, out_weight, gate):
    hidden, q, k, v = hidden_in[0], queries[0], keys[0], values[0]
    tok, _ = q.shape
    seq = ("yv", "z", "xh")
    rows = tok // 2
    n = 2 * HEADS

    (away,) = pack(pack_send_kernel, [(3, HEADS, rows, HD)], q, k, v)
    came = lax.ppermute(away, "c", SWAP)
    (mine,) = pack(pack_keep_kernel, [(2, 1, HEADS, 3, rows, HD)], q, k, v)
    mine = place(mine, came)
    got = lax.all_to_all(mine.reshape(n, 3 * rows, HD), seq, split_axis=0, concat_axis=0, tiled=True)
    got = got.reshape(n, 3, rows, HD)

    step, half = n // CHUNKS, n // 2
    own = [got[i * step : (i + 1) * step, 1:] for i in range(CHUNKS)]
    own_pair = swap(own, "c")
    qs = [got[a * n // 4 : b * n // 4, 0] for a, b in ((0, 1), (1, 2), (2, 4))]
    here, got = lax.optimization_barrier((mine, got))
    other = lax.ppermute(here[:, :, :, 1:], "xl", SWAP)
    mate_q1 = lax.ppermute(got[:half, 0], "yr", SWAP)

    o1, l1, keys_all, values_all = attend(qs[0], own + own_pair, True, False)
    kv = keys_all, values_all
    q_in, q2, o1 = lax.optimization_barrier((qs[1], got[half:, 0], o1))
    mate_q2 = lax.ppermute(q2, "yr", SWAP)
    o2, l2 = attend(q_in, kv, False, False)
    q_in, o2 = lax.optimization_barrier((mate_q1, o2))
    (mo1,) = attend(q_in, kv, False, True)
    back1 = lax.ppermute(mo1, "yr", SWAP)
    q_in, mo1 = lax.optimization_barrier((mate_q2, mo1))
    (mo2,) = attend(q_in, kv, False, True)
    back2 = lax.ppermute(mo2, "yr", SWAP)
    q_in, back1, mo2 = lax.optimization_barrier((qs[2], back1, mo2))
    o3, l3 = attend(q_in, kv, False, False)
    other, o3 = lax.optimization_barrier((other, o3))
    cross_send = cross(mine, other, None, True)
    back2, cross_send = lax.optimization_barrier((back2, cross_send))
    o = merge([(o1, l1), (o2, l2), (o3, l3)], [back1, back2])
    back = lax.all_to_all(o, seq, split_axis=0, concat_axis=0, tiled=True)
    here, back = lax.optimization_barrier((mine, back))
    back = back.reshape(mine.shape[:3] + (rows, HD))
    send = add_send(back, cross_send)
    came = lax.ppermute(send, "c", SWAP)
    keep = cross(here, other, back, False)
    return project(keep, came, out_weight, hidden, gate)[None]


def solution(mesh):
    devices = np.asarray(mesh.devices)
    fine = Mesh(devices.reshape(2, 2, 2, 2, 8, 2), ("xl", "c", "yv", "yr", "z", "xh"))
    view, seq = ("xl", "c"), ("yv", "yr", "z", "xh")
    spec = P(view, seq, None)
    return jax.shard_map(
        local,
        mesh=fine,
        in_specs=(spec, spec, spec, spec, P(), P(view, None)),
        out_specs=spec,
        check_vma=False,
    )
```

```python
import functools
import math

import jax
import jax.numpy as jnp
import numpy as np
from jax import lax
from jax.experimental import pallas as pl
from jax.experimental.pallas import tpu as pltpu
from jax.sharding import Mesh, PartitionSpec as P

HEADS = 16
HD = 128
BF = jnp.bfloat16
F32 = jnp.float32
SCALE = HD**-0.5
LOG2E = math.log2(math.e)
NT = (((1,), (1,)), ((), ()))
VMEM_CAP = 30 * 2**20


def params(**kw):
    return pltpu.CompilerParams(vmem_limit_bytes=VMEM_CAP, **kw)


def whole(n):
    return [pl.BlockSpec(memory_space=pltpu.VMEM)] * n


def fetch_half(core, refs, held, sems):
    half = held.shape[1]
    part = pl.ds(pl.multiple_of(core * half, half), half)
    moves = [
        pltpu.make_async_copy(ref.at[part], held.at[j], sems.at[j]) for j, ref in enumerate(refs)
    ]
    for move in moves:
        move.start()
    return moves


def pack_send_kernel(q_ref, k_ref, v_ref, o_ref, held, sems):
    moves = fetch_half(1 - lax.axis_index("c"), (q_ref, k_ref, v_ref), held, sems)
    for j in range(3):
        moves[j].wait()
        for h in range(o_ref.shape[1]):
            o_ref[j, h] = held[j, :, h * HD : (h + 1) * HD]


def pack_keep_kernel(q_ref, k_ref, v_ref, o_ref, held, sems):
    me = lax.axis_index("c")
    moves = fetch_half(me, (q_ref, k_ref, v_ref), held, sems)
    for j in range(3):
        moves[j].wait()
        for h in range(o_ref.shape[2]):
            o_ref[me, 0, h, j] = held[j, :, h * HD : (h + 1) * HD]


def pack(kernel, out_shape, q, k, v):
    tok, width = q.shape
    return pl.pallas_call(
        kernel,
        in_specs=[pl.BlockSpec(memory_space=pltpu.HBM)] * 3,
        out_specs=whole(len(out_shape)),
        out_shape=[jax.ShapeDtypeStruct(x, BF) for x in out_shape],
        scratch_shapes=[pltpu.VMEM((3, tok // 2, width), BF), pltpu.SemaphoreType.DMA((3,))],
        compiler_params=params(),
        name="pack",
    )(*(pltpu.with_memory_space_constraint(x, pltpu.HBM) for x in (q, k, v)))


def place_kernel(a_ref, got_ref, o_ref):
    you = 1 - lax.axis_index("c")
    for j in range(got_ref.shape[0]):
        for h in range(got_ref.shape[1]):
            o_ref[you, 0, h, j] = got_ref[j, h]


def place(mine, got):
    return pl.pallas_call(
        place_kernel,
        in_specs=whole(2),
        out_specs=pl.BlockSpec(memory_space=pltpu.VMEM),
        out_shape=jax.ShapeDtypeStruct(mine.shape, BF),
        input_output_aliases={0: 0},
        compiler_params=params(),
        name="place",
    )(mine, got)


def gather_kv(kv_refs, k_all, v_all):
    at = 0
    for ref in kv_refs:
        n = ref.shape[0] * ref.shape[2]
        k_all[at : at + n, :] = ref[:, 0].reshape(n, HD)
        v_all[at : at + n, :HD] = ref[:, 1].reshape(n, HD)
        at += n
    v_all[:, HD:] = jnp.ones((at, HD), BF)


def eye():
    shape = (HD, HD)
    return lax.broadcasted_iota(jnp.int32, shape, 0) == lax.broadcasted_iota(jnp.int32, shape, 1)


def attend_block(q, k_all, v_all, kb):
    c = SCALE * LOG2E
    total = k_all.shape[0]

    def score(i):
        return lax.dot_general(q, k_all[i * kb : (i + 1) * kb, :], NT, preferred_element_type=F32)

    m = acc = None
    s = score(0)
    for i in range(total // kb):
        following = score(i + 1) if (i + 1) * kb < total else None
        peak = jnp.max(s, axis=1, keepdims=True) * c
        new = peak if m is None else jnp.maximum(m, peak)
        p = jnp.exp2(s * c - new).astype(BF)
        add = jnp.dot(p, v_all[i * kb : (i + 1) * kb, :], preferred_element_type=F32)
        acc = add if acc is None else acc * jnp.exp2(m - new) + add
        m, s = new, following
    return acc[:, :HD] / acc[:, HD:], m + jnp.log2(acc[:, HD:])


def attend_kernel(*refs, first, travels, qb, kb):
    if first:
        q_ref, *kv_refs, o_ref, l_ref, k_all, v_all = refs
        gather_kv(kv_refs, k_all, v_all)
    else:
        q_ref, k_all, v_all, o_ref, l_ref = refs
    src, rows, _ = q_ref.shape
    qsrc = qb // rows
    diag = eye()
    for j in range(src // qsrc):
        q = q_ref[j * qsrc : (j + 1) * qsrc].reshape(qb, HD)
        o, lse = attend_block(q, k_all, v_all, kb)
        o_ref[j * qsrc : (j + 1) * qsrc] = o.reshape(qsrc, rows, HD).astype(o_ref.dtype)
        for g in range(qb // HD):
            line = jnp.where(diag, lse[g * HD : (g + 1) * HD], 0.0)
            l_ref[j * (qb // HD) + g, :] = jnp.sum(line, axis=0)
    if travels:
        lines = l_ref.shape[0]
        lse = l_ref[...]
        terms = []
        for _ in range(3):
            terms.append(lse.astype(BF))
            lse = lse - terms[-1].astype(F32)
        terms.append(jnp.zeros((rows - 3 * lines, HD), BF))
        o_ref[src] = jnp.concatenate(terms, axis=0)


def attend(q, kv, first, travels, kb=2048):
    src, rows, _ = q.shape
    nq = src * rows
    qb = nq if nq <= 512 else nq // 2
    total = sum(a.shape[0] * a.shape[2] for a in kv) if first else kv[0].shape[0]
    out_shape = [jax.ShapeDtypeStruct((src + travels, rows, HD), BF if travels else F32)]
    if not travels:
        out_shape.append(jax.ShapeDtypeStruct((nq // HD, HD), F32))
    if first:
        out_shape += [
            jax.ShapeDtypeStruct((total, HD), BF),
            jax.ShapeDtypeStruct((total, 2 * HD), BF),
        ]
    return pl.pallas_call(
        functools.partial(attend_kernel, first=first, travels=travels, qb=qb, kb=min(kb, total)),
        in_specs=whole(1 + len(kv)),
        out_specs=whole(len(out_shape)),
        out_shape=out_shape,
        scratch_shapes=[pltpu.VMEM((nq // HD, HD), F32)] if travels else [],
        compiler_params=params(),
        cost_estimate=pl.CostEstimate(
            flops=0,
            bytes_accessed=0,
            transcendentals=0,
        ),
        name="attend",
    )(q, *kv)


def merge_kernel(*refs, own_parts):
    *refs, out_ref = refs
    diag = eye()
    rows = out_ref.shape[1]
    per = HD // rows
    here, there = [], []
    for o_ref, l_ref in zip(refs[: 2 * own_parts : 2], refs[1 : 2 * own_parts : 2]):
        for g in range(l_ref.shape[0]):
            here.append((o_ref, g, l_ref[g : g + 1, :]))
    for o_ref in refs[2 * own_parts :]:
        src = o_ref.shape[0] - 1
        lines = src // per
        terms = o_ref[src].astype(F32)
        lse = terms[:lines] + terms[lines : 2 * lines] + terms[2 * lines : 3 * lines]
        for g in range(lines):
            there.append((o_ref, g, lse[g : g + 1, :]))
    for i, ((oa, ga, la), (ob, gb, lb)) in enumerate(zip(here, there)):
        peak = jnp.maximum(la, lb)
        ea, eb = jnp.exp2(la - peak), jnp.exp2(lb - peak)
        w = jnp.sum(jnp.where(diag, ea / (ea + eb), 0.0), axis=1, keepdims=True)
        a = oa[ga * per : (ga + 1) * per].reshape(HD, HD)
        b = ob[gb * per : (gb + 1) * per].reshape(HD, HD).astype(F32)
        out_ref[i * per : (i + 1) * per] = (b + w * (a - b)).astype(BF).reshape(per, rows, HD)


def merge(own, travelled):
    src = sum(o.shape[0] for o, _ in own)
    flat = [x for p in own for x in p] + travelled
    return pl.pallas_call(
        functools.partial(merge_kernel, own_parts=len(own)),
        in_specs=whole(len(flat)),
        out_specs=pl.BlockSpec(memory_space=pltpu.VMEM),
        out_shape=jax.ShapeDtypeStruct((src,) + own[0][0].shape[1:], BF),
        compiler_params=params(),
        name="merge",
    )(*flat)


def cross_kernel(a_ref, b_ref, *refs, flip):
    *s_ref, o_ref = refs
    views, parts, heads = a_ref.shape[:3]
    view = lax.axis_index("c")
    if flip:
        view = 1 - view

    def one_head(h, carry):
        for r in range(parts):
            ks = [a_ref[b, r, h, 1].astype(F32) for b in range(views)]
            ks += [b_ref[b, r, h, 0].astype(F32) for b in range(views)]
            vs = [a_ref[b, r, h, 2].astype(F32) for b in range(views)]
            vs += [b_ref[b, r, h, 1].astype(F32) for b in range(views)]
            q = a_ref[view, r, h, 0].astype(F32)
            s = [jnp.sum(q * k, axis=1, keepdims=True) * SCALE for k in ks]
            peak = functools.reduce(jnp.maximum, s)
            e = [jnp.exp(x - peak) for x in s]
            inv = 1.0 / functools.reduce(jnp.add, e)
            terms = [(x * inv).astype(BF).astype(F32) * v for x, v in zip(e, vs)]
            out = functools.reduce(jnp.add, terms)
            if s_ref:
                out = s_ref[0][view, r, h].astype(F32) + out
            o_ref[r, h] = out.astype(o_ref.dtype)
        return carry

    lax.fori_loop(0, heads, one_head, 0, unroll=8)


def cross(mine, other, back, flip):
    args = (mine, other) if back is None else (mine, other, back)
    out = jax.ShapeDtypeStruct(mine.shape[1:3] + mine.shape[4:], F32 if back is None else BF)
    return pl.pallas_call(
        functools.partial(cross_kernel, flip=flip),
        in_specs=whole(len(args)),
        out_specs=pl.BlockSpec(memory_space=pltpu.VMEM),
        out_shape=out,
        compiler_params=params(),
        name="cross",
    )(*args)


def add_kernel(s_ref, c_ref, o_ref):
    o_ref[...] = (s_ref[1 - lax.axis_index("c")].astype(F32) + c_ref[...]).astype(BF)


def add_send(back, cross_out):
    return pl.pallas_call(
        add_kernel,
        in_specs=whole(2),
        out_specs=pl.BlockSpec(memory_space=pltpu.VMEM),
        out_shape=jax.ShapeDtypeStruct(cross_out.shape, BF),
        compiler_params=params(),
        name="add_send",
    )(back, cross_out)


def project_kernel(keep_ref, came_ref, w_ref, h_ref, g_ref, o_ref, att):
    half = o_ref.shape[0] // 2
    me = lax.axis_index("c")
    for core, ref in ((me, keep_ref), (1 - me, came_ref)):
        parts, heads, rows, _ = ref.shape
        for r in range(parts):
            at = pl.ds(pl.multiple_of(core * half + r * rows, rows), rows)
            for h in range(heads):
                att[at, h * HD : (h + 1) * HD] = ref[r, h]
    nb = 512
    for i in range(o_ref.shape[1] // nb):
        cols = slice(i * nb, (i + 1) * nb)
        y = jnp.dot(att[...], w_ref[:, cols], preferred_element_type=F32)
        o_ref[:, cols] = (h_ref[:, cols].astype(F32) + g_ref[:, cols].astype(F32) * y).astype(BF)


def project(keep, came, w, hidden, gate):
    return pl.pallas_call(
        project_kernel,
        in_specs=whole(5),
        out_specs=pl.BlockSpec(memory_space=pltpu.VMEM),
        out_shape=jax.ShapeDtypeStruct(hidden.shape, BF),
        scratch_shapes=[pltpu.VMEM(hidden.shape, BF)],
        compiler_params=params(),
        name="project",
    )(keep, came, w, hidden, gate)


SWAP = [(0, 1), (1, 0)]
CHUNKS = 1


def swap(chunks, axis):
    return [lax.ppermute(x, axis, SWAP) for x in chunks]


def local(hidden_in, queries, keys, values, out_weight, gate):
    hidden, q, k, v = hidden_in[0], queries[0], keys[0], values[0]
    tok, _ = q.shape
    seq = ("yv", "z", "xh")
    rows = tok // 2
    n = 2 * HEADS

    (away,) = pack(pack_send_kernel, [(3, HEADS, rows, HD)], q, k, v)
    came = lax.ppermute(away, "c", SWAP)
    (mine,) = pack(pack_keep_kernel, [(2, 1, HEADS, 3, rows, HD)], q, k, v)
    mine = place(mine, came)
    got = lax.all_to_all(mine.reshape(n, 3 * rows, HD), seq, split_axis=0, concat_axis=0, tiled=True)
    got = got.reshape(n, 3, rows, HD)

    step, half = n // CHUNKS, n // 2
    own = [got[i * step : (i + 1) * step, 1:] for i in range(CHUNKS)]
    own_pair = swap(own, "c")
    qs = [got[a * n // 4 : b * n // 4, 0] for a, b in ((0, 1), (1, 2), (2, 4))]
    here, got = lax.optimization_barrier((mine, got))
    other = lax.ppermute(here[:, :, :, 1:], "xl", SWAP)
    mate_q1 = lax.ppermute(got[:half, 0], "yr", SWAP)

    o1, l1, keys_all, values_all = attend(qs[0], own + own_pair, True, False)
    kv = keys_all, values_all
    q_in, q2, o1 = lax.optimization_barrier((qs[1], got[half:, 0], o1))
    mate_q2 = lax.ppermute(q2, "yr", SWAP)
    o2, l2 = attend(q_in, kv, False, False)
    q_in, o2 = lax.optimization_barrier((mate_q1, o2))
    (mo1,) = attend(q_in, kv, False, True)
    back1 = lax.ppermute(mo1, "yr", SWAP)
    q_in, mo1 = lax.optimization_barrier((mate_q2, mo1))
    (mo2,) = attend(q_in, kv, False, True)
    back2 = lax.ppermute(mo2, "yr", SWAP)
    q_in, mo2 = lax.optimization_barrier((qs[2], mo2))
    o3, l3 = attend(q_in, kv, False, False)
    other, back1, o3 = lax.optimization_barrier((other, back1, o3))
    cross_send = cross(mine, other, None, True)
    back2, cross_send = lax.optimization_barrier((back2, cross_send))
    o = merge([(o1, l1), (o2, l2), (o3, l3)], [back1, back2])
    back = lax.all_to_all(o, seq, split_axis=0, concat_axis=0, tiled=True)
    here, back = lax.optimization_barrier((mine, back))
    back = back.reshape(mine.shape[:3] + (rows, HD))
    send = add_send(back, cross_send)
    came = lax.ppermute(send, "c", SWAP)
    keep = cross(here, other, back, False)
    return project(keep, came, out_weight, hidden, gate)[None]


def solution(mesh):
    devices = np.asarray(mesh.devices)
    fine = Mesh(devices.reshape(2, 2, 2, 2, 8, 2), ("xl", "c", "yv", "yr", "z", "xh"))
    view, seq = ("xl", "c"), ("yv", "yr", "z", "xh")
    spec = P(view, seq, None)
    return jax.shard_map(
        local,
        mesh=fine,
        in_specs=(spec, spec, spec, spec, P(), P(view, None)),
        out_specs=spec,
        check_vma=False,
    )
```
